128 devices in a mesh: row: 16 (over z_lo, x, core), col: 8 (over y, z_hi).
Axes of the slice: x: 4, y: 4, z: 4 (z_hi: 2, z_lo: 2; z = z_hi * 2 + z_lo), core: 2. Of those that a mesh axis runs over, the one named last changes fastest.
Arguments:
- inputs: bfloat16 [2048, 8192], P('row', 'col'), may hold values from -0.875 to 0.875
- upstream: bfloat16 [2048, 8192], P('row', 'col'), may hold values from -0.75 to 0.75
- mask_flags: int32 [2048], P('row'), may hold values from 0 to 1, as said below
- levels: int32 [4], replicated, may hold values from 100 to 1000
- gate_saved: bfloat16 [2048, 14336], P('col', 'row'), may hold values from -8 to 8
- up_saved: bfloat16 [2048, 14336], P('col', 'row'), may hold values from -3 to 3
- gate_weight: bfloat16 [8192, 14336], P('col', 'row'), may hold values from -0.0625 to 0.0625
- up_weight: bfloat16 [8192, 14336], P('col', 'row'), may hold values from -0.0625 to 0.0625
- down_weight: bfloat16 [14336, 8192], P('row', 'col'), may hold values from -0.046875 to 0.046875
Outputs:
- grad_input: bfloat16 [2048, 8192], P('row', 'col')
- grad_gate: bfloat16 [8192, 14336], P('col', 'row')
- grad_up: bfloat16 [8192, 14336], P('col', 'row')
- grad_down: bfloat16 [14336, 8192], P('row', 'col')
The draws below stay inside these ranges and needn't reach their ends.
Inputs may be any that keep to these rules, and one draw needn't show every extreme that they name: `mask_flags`: the first token of every sequence is masked.
All inputs are finite; a program needn't handle non-finite values.
Results may differ from the reference program's by a relative error of at most 0.03.
Values may be sent and summed in bfloat16 or wider, within the bound.
A program may use at most 128 MiB of HBM per device.

```python
import jax
import jax.numpy as jnp
from jax import lax

D = 8192
FF = 14336
SEQ = 512
TOKENS = 2048
NSEQ = 4
FEAT_BLOCK = 1024
HID_BLOCK = 896
N_ROW = 16
N_COL = 8


def draw_mask_flags(key, part):
    key = jax.random.fold_in(key, 7)
    position = jnp.arange(TOKENS, dtype=jnp.int32)
    ticket = jax.random.randint(key, (TOKENS,), 0, 4 * TOKENS, dtype=jnp.int32)
    masked = (ticket < TOKENS + 2 * position) | (position % SEQ == 0)
    return masked.astype(jnp.int32)


def touch_ends(drawn, key, low, largest):
    extent = drawn.shape
    spot = [jax.random.randint(jax.random.fold_in(key, axis), (), 0, extent[axis]) for axis in range(len(extent))]
    drawn = drawn.at[tuple(spot)].set(low)
    longest = extent.index(max(extent))
    spot[longest] = (spot[longest] + 1) % extent[longest]
    return drawn.at[tuple(spot)].set(largest)


def level_of(key, shape, pieces, low, high):
    def one(dim, parts):
        steps = jax.random.uniform(jax.random.fold_in(jax.random.fold_in(key, 6), dim), (parts,), jnp.float32, low / len(pieces), high / len(pieces))
        return jnp.repeat(jnp.exp(steps), shape[dim] // parts).reshape((-1,) + (1,) * (len(shape) - dim - 1))

    factor_of = one(*pieces[0])
    for cut in pieces[1:]:
        factor_of = factor_of * one(*cut)
    return factor_of


def bell_draw(own_key, extent, width, reach, cuts=(), kind=jnp.bfloat16):
    gain = level_of(own_key, extent, cuts, -0.22, 0.18) if cuts else 1.0
    drawn = jax.random.normal(own_key, extent, jnp.float32) * width * gain
    return jnp.minimum(jnp.maximum(drawn, -reach), reach).astype(kind)


def setup_inputs(seed: int = 0) -> dict:
    splits = jax.random.split(jax.random.key(seed), 10)
    return {
        "inputs": bell_draw(splits[0], (TOKENS, D), 0.15, 0.875, ((0, 16), (1, 8))),
        "upstream": bell_draw(splits[1], (TOKENS, D), 0.125, 0.75, ((0, 16), (1, 8))),
        "mask_flags": draw_mask_flags(jax.random.fold_in(splits[9], 71), 0),
        "levels": touch_ends(jax.random.randint(splits[3], (NSEQ,), 100, 1001), jax.random.fold_in(splits[3], 1), 100, 1000).astype(jnp.int32),
        "gate_saved": bell_draw(splits[4], (TOKENS, FF), 1.5, 8.0, ((0, 8), (1, 16))),
        "up_saved": bell_draw(splits[5], (TOKENS, FF), 0.5, 3.0, ((0, 8), (1, 16))),
        "gate_weight": bell_draw(splits[6], (D, FF), D ** -0.5, 0.0625, ((0, 8), (1, 16))),
        "up_weight": bell_draw(splits[7], (D, FF), D ** -0.5, 0.0625, ((0, 8), (1, 16))),
        "down_weight": bell_draw(splits[8], (FF, D), FF ** -0.5, 0.046875, ((0, 16), (1, 8))),
    }


def hidden_side(hidden_grad, gate_vals, up_vals):
    gate_f = gate_vals.astype(jnp.float32)
    up_f = up_vals.astype(jnp.float32)
    sigmoid_gate = jax.nn.sigmoid(gate_f)
    silu_gate = sigmoid_gate * gate_f
    hidden = (silu_gate * up_f).astype(jnp.bfloat16)
    gate_grad = (hidden_grad * up_f * sigmoid_gate * (1.0 + gate_f * (1.0 - sigmoid_gate))).astype(jnp.bfloat16)
    up_grad = (hidden_grad * silu_gate).astype(jnp.bfloat16)
    return hidden, gate_grad, up_grad


def reference(inputs, upstream, mask_flags, levels, gate_saved, up_saved, gate_weight, up_weight, down_weight):
    noise_level = levels.astype(jnp.float32) / 1000.0
    masked_total = jnp.sum(mask_flags.astype(jnp.float32))
    loss_scale = jnp.float32(TOKENS) / masked_total
    position = jnp.arange(TOKENS, dtype=jnp.int32)
    token_noise = noise_level[position // SEQ]
    factor = mask_flags.astype(jnp.float32) / token_noise
    weighted = (upstream.astype(jnp.float32) * factor[:, None]).astype(jnp.bfloat16)
    weighted_blocks = weighted.reshape(TOKENS, N_COL, FEAT_BLOCK)
    down_blocks = down_weight.reshape(FF, N_COL, FEAT_BLOCK)
    contract_last = (((1,), (1,)), ((), ()))
    contract_first = (((0,), (0,)), ((), ()))

    def add_block(running, block_index):
        weighted_block = lax.dynamic_index_in_dim(weighted_blocks, block_index, 1, keepdims=False)
        down_block = lax.dynamic_index_in_dim(down_blocks, block_index, 1, keepdims=False)
        partial_term = lax.dot_general(weighted_block, down_block, contract_last, preferred_element_type=jnp.float32)
        rounded = lax.optimization_barrier(partial_term.astype(jnp.bfloat16))
        return running + rounded.astype(jnp.float32), None

    running = lax.scan(add_block, jnp.zeros((TOKENS, FF), jnp.float32), jnp.arange(N_COL, dtype=jnp.int32))[0]
    hidden_grad = loss_scale * running
    hidden, gate_grad, up_grad = hidden_side(hidden_grad, gate_saved, up_saved)
    grad_down = (loss_scale * lax.dot_general(hidden, weighted, contract_first, preferred_element_type=jnp.float32)).astype(jnp.bfloat16)
    grad_gate = lax.dot_general(inputs, gate_grad, contract_first, preferred_element_type=jnp.float32).astype(jnp.bfloat16)
    grad_up = lax.dot_general(inputs, up_grad, contract_first, preferred_element_type=jnp.float32).astype(jnp.bfloat16)
    gate_grad_blocks = gate_grad.reshape(TOKENS, N_ROW, HID_BLOCK)
    up_grad_blocks = up_grad.reshape(TOKENS, N_ROW, HID_BLOCK)
    gate_weight_blocks = gate_weight.reshape(D, N_ROW, HID_BLOCK)
    up_weight_blocks = up_weight.reshape(D, N_ROW, HID_BLOCK)

    def add_hidden_block(running_input, block_index):
        gate_rows = lax.dynamic_index_in_dim(gate_grad_blocks, block_index, 1, keepdims=False)
        up_rows = lax.dynamic_index_in_dim(up_grad_blocks, block_index, 1, keepdims=False)
        gate_cols = lax.dynamic_index_in_dim(gate_weight_blocks, block_index, 1, keepdims=False)
        up_cols = lax.dynamic_index_in_dim(up_weight_blocks, block_index, 1, keepdims=False)
        term = lax.dot_general(gate_rows, gate_cols, contract_last, preferred_element_type=jnp.float32) + lax.dot_general(up_rows, up_cols, contract_last, preferred_element_type=jnp.float32)
        rounded = lax.optimization_barrier(term.astype(jnp.bfloat16))
        return running_input + rounded.astype(jnp.float32), None

    input_sum = lax.scan(add_hidden_block, jnp.zeros((TOKENS, D), jnp.float32), jnp.arange(N_ROW, dtype=jnp.int32))[0]
    grad_input = input_sum.astype(jnp.bfloat16)
    return (grad_input, grad_gate, grad_up, grad_down)
```

```python
import jax
import jax.numpy as jnp
from jax import lax
from jax.experimental import pallas as pl
from jax.experimental.pallas import tpu as pltpu
from jax.sharding import PartitionSpec as P

SEQ = 512
BF = jnp.bfloat16
F32 = jnp.float32
MESH = pl.DeviceIdType.MESH
NT = (((1,), (1,)), ((), ()))
ORDER = ((2, 1), (2, 0), (1, 1), (-1, 1), (1, 0), (-1, 0), (0, 1), (0, 0))


class Wire:
    def __init__(self, send_sems, recv_sems, anyone):
        self.send_sems, self.recv_sems, self.anyone = send_sems, recv_sems, anyone
        self.count = 0
        self.sent = []

    def new(self):
        self.count += 1
        return self.count - 1

    def copy(self, number, src, dst, device):
        return pltpu.make_async_remote_copy(
            src_ref=src,
            dst_ref=dst,
            send_sem=self.send_sems.at[number],
            recv_sem=self.recv_sems.at[number],
            device_id=device,
            device_id_type=MESH,
        )

    def send(self, number, src, dst, device, keep=True):
        self.copy(number, src, dst, device).start()
        if keep:
            self.sent.append((number, src, dst, device))

    def recv(self, number, dst):
        self.copy(number, dst, dst, self.anyone).wait_recv()

    def drain(self):
        for message in self.sent:
            self.copy(*message).wait_send()


class Gather:
    def __init__(self, wire, buf, slot, minus, plus, across, sibling=None, other_slot=None):
        self.wire, self.buf, self.slot = wire, buf, slot
        self.minus, self.plus, self.across = minus, plus, across
        self.sibling, self.other_slot = sibling, other_slot
        self.ids = {
            name: wire.new()
            for name in ("own_m", "own_p", "own_z", "z_m", "z_p", "fwd_p", "opp_z")
        }
        self.sib_ids = {d: wire.new() for d in ORDER} if sibling is not None else {}

    def push(self, name, d, device):
        ref = self.buf.at[self.slot(d)]
        self.wire.send(self.ids[name], ref, ref, device)

    def share(self, d):
        if self.sibling is not None:
            ref = self.buf.at[self.slot(d)]
            self.wire.send(self.sib_ids[d], ref, ref, self.sibling)

    def take(self, name, d):
        self.wire.recv(self.ids[name], self.buf.at[self.slot(d)])

    def start(self):
        self.push("own_z", (0, 0), self.across)
        self.push("own_m", (0, 0), self.minus)
        self.push("own_p", (0, 0), self.plus)
        self.share((0, 0))

    def z1(self):
        self.take("own_z", (0, 1))
        self.push("z_m", (0, 1), self.minus)
        self.push("z_p", (0, 1), self.plus)
        self.share((0, 1))

    def f1(self):
        self.take("own_p", (-1, 0))
        self.push("fwd_p", (-1, 0), self.plus)
        self.share((-1, 0))

    def rest(self):
        self.take("own_m", (1, 0))
        self.share((1, 0))
        self.take("z_p", (-1, 1))
        self.share((-1, 1))
        self.take("z_m", (1, 1))
        self.share((1, 1))

    def g1(self):
        self.take("fwd_p", (2, 0))
        self.push("opp_z", (2, 0), self.across)
        self.share((2, 0))

    def last(self):
        self.take("opp_z", (2, 1))
        self.share((2, 1))

    def from_sibling(self):
        for d in ORDER:
            self.wire.recv(self.sib_ids[d], self.buf.at[self.other_slot(d)])


class Reduce:
    def __init__(self, wire, part, got, minus, plus, across, keep=True):
        self.wire, self.part, self.got = wire, part, got
        self.minus, self.plus, self.across, self.keep = minus, plus, across, keep
        self.ids = [wire.new() for _ in range(7)]
        self.log = []

    def push(self, index, d, device):
        src = self.part.at[ORDER.index(d)]
        message = (self.ids[index], src, self.got.at[index], device)
        self.wire.send(*message, keep=self.keep)
        self.log.append((index, d, device))

    def drain(self):
        for index, d, device in self.log:
            src = self.part.at[ORDER.index(d)]
            self.wire.copy(self.ids[index], src, self.got.at[index], device).wait_send()

    def add(self, d, *indices):
        term = self.part[ORDER.index(d)].astype(F32)
        for index in indices:
            self.wire.recv(self.ids[index], self.got.at[index])
            term = term + self.got[index].astype(F32)
        return term

    def store(self, d, term):
        self.part[ORDER.index(d)] = term.astype(BF)

    def p0(self):
        self.push(0, (2, 1), self.across)

    def p1(self):
        self.push(2, (1, 1), self.plus)
        self.push(3, (-1, 1), self.minus)

    def p2(self):
        self.push(4, (1, 0), self.plus)

    def t20(self):
        self.store((2, 0), self.add((2, 0), 0))
        self.push(1, (2, 0), self.minus)

    def tm10(self):
        self.store((-1, 0), self.add((-1, 0), 1))
        self.push(5, (-1, 0), self.minus)

    def s01(self):
        self.store((0, 1), self.add((0, 1), 2, 3))
        self.push(6, (0, 1), self.across)

    def final(self):
        return self.add((0, 0), 4, 6, 5)


N_MESSAGES = 2 * 15 + 3 * 2 * 7 + 2 * 7 + 2 * (8 + 7) + 4
N_LOCAL = 10


def kernel(
    levels,
    mask_row,
    inputs,
    upstream,
    gate_saved,
    up_saved,
    gate_weight,
    up_weight,
    down_weight,
    grad_input,
    grad_gate,
    grad_up,
    grad_down,
    w_all,
    in_all,
    h_all,
    g_all,
    u_all,
    gw,
    uw,
    dw,
    up_own,
    in_own,
    gs,
    us,
    h_part,
    h_got,
    q_part,
    q_sib,
    q_got,
    acc_gate,
    acc_up,
    out_gate,
    out_up,
    out_down,
    out_in,
    count,
    send_sems,
    recv_sems,
    local_sems,
):
    row, col = lax.axis_index("row"), lax.axis_index("col")
    z_lo, x, core = row // 8, (row // 2) % 4, row % 2
    y, z_hi = col // 2, col % 2
    sign = 1 - 2 * core

    def row_of(z, x_at, k):
        return z * 8 + lax.rem(x_at + 8, 4) * 2 + k

    def col_of(y_at, z):
        return lax.rem(y_at + 8, 4) * 2 + z

    sibling = (row_of(z_lo, x, 1 - core), col)
    row_z = (row_of(1 - z_lo, x, core), col)
    row_m, row_p = (row_of(z_lo, x - sign, core), col), (row_of(z_lo, x + sign, core), col)
    col_z = (row, col_of(y, 1 - z_hi))
    col_m, col_p = (row, col_of(y - sign, z_hi)), (row, col_of(y + sign, z_hi))

    def flip(bit, d):
        return 1 - bit if d else bit

    def row_slot(d, k=core):
        return row_of(flip(z_lo, d[1]), x + sign * d[0], k)

    def col_slot(d, half):
        return 2 * col_of(y + sign * d[0], flip(z_hi, d[1])) + half

    loads = {}
    for number, (name, src, dst) in enumerate(
        (
            ("upstream", upstream, up_own),
            ("gs", gate_saved, gs),
            ("us", up_saved, us),
            ("inputs", inputs, in_own),
            ("dw", down_weight, dw),
            ("gw", gate_weight, gw),
            ("uw", up_weight, uw),
        )
    ):
        loads[name] = pltpu.make_async_copy(src, dst, local_sems.at[number])
        loads[name].start()

    barrier = pltpu.get_barrier_semaphore()
    neighbours = (sibling, row_z, row_m, row_p, col_z, col_m, col_p)
    for device in neighbours:
        pl.semaphore_signal(barrier, inc=1, device_id=device, device_id_type=MESH)

    flags = jnp.transpose(jnp.broadcast_to(mask_row[...].astype(F32), (128, 128)))
    noise = jnp.full((1, 128), levels[row * 128 // SEQ], jnp.int32).astype(F32) / 1000.0
    factor = flags / noise
    loads["upstream"].wait()
    w_all[row] = (up_own[...].astype(F32) * jnp.concatenate([factor] * 8, axis=1)).astype(BF)
    count[0] = jnp.broadcast_to(jnp.sum(flags, axis=0, keepdims=True), (8, 128))

    pl.semaphore_wait(barrier, len(neighbours))

    wire = Wire(send_sems, recv_sems, sibling)
    gather_w = Gather(wire, w_all, row_slot, row_m, row_p, row_z, sibling, lambda d: row_slot(d, 1 - core))
    gather_i = Gather(wire, in_all, row_slot, row_m, row_p, row_z, sibling, lambda d: row_slot(d, 1 - core))

    def col_gather(buf, half):
        return Gather(wire, buf, lambda d: col_slot(d, half), col_m, col_p, col_z)

    gather_h = [col_gather(h_all, half) for half in range(2)]
    gather_g = [col_gather(g_all, half) for half in range(2)]
    gather_u = [col_gather(u_all, half) for half in range(2)]
    reduce_h = [Reduce(wire, h_part.at[half], h_got.at[half], col_m, col_p, col_z) for half in range(2)]

    step = 1 - 2 * lax.rem(x, 2)
    partners = (
        sibling,
        row_z,
        (row_of(z_lo, x + step, core), col),
        (row_of(z_lo, x - step, core), col),
    )
    count_ids = [wire.new() for _ in partners]

    def count_send(stage):
        wire.send(count_ids[stage], count.at[2 * stage], count.at[2 * stage + 1], partners[stage])

    def count_recv(stage):
        wire.recv(count_ids[stage], count.at[2 * stage + 1])
        count[2 * stage + 2] = count[2 * stage] + count[2 * stage + 1]

    gather_w.start()
    count_send(0)

    def saved(half):
        gate_f = gs[pl.ds(half * 128, 128), :].astype(F32)
        up_f = us[pl.ds(half * 128, 128), :].astype(F32)
        sigmoid_gate = jax.nn.sigmoid(gate_f)
        return gate_f, up_f, sigmoid_gate, sigmoid_gate * gate_f

    loads["gs"].wait()
    loads["us"].wait()
    for half in range(2):
        _, up_f, _, silu_gate = saved(half)
        hidden = (silu_gate * up_f).astype(BF).astype(F32)
        h_all[2 * col + half] = jnp.transpose(hidden).astype(BF)
        gather_h[half].start()
    loads["inputs"].wait()
    in_all[row] = jnp.transpose(in_own[...].astype(F32)).astype(BF)

    gather_w.z1()
    gather_h[0].z1()
    gather_w.f1()
    count_recv(0)
    count_send(1)
    gather_h[1].z1()
    gather_w.rest()
    gather_h[0].f1()
    gather_w.g1()
    gather_h[1].f1()
    gather_h[0].rest()
    gather_w.last()
    gather_w.from_sibling()
    gather_i.start()
    count_recv(1)
    count_send(2)
    loads["dw"].wait()

    def terms(half, pair):
        ds = ORDER[2 * pair : 2 * pair + 2]
        rows = jnp.concatenate([w_all[col_slot(d, half)] for d in ds], axis=0)
        term = lax.dot_general(rows, dw[...], NT, preferred_element_type=F32).astype(BF)
        h_part[half, 2 * pair] = term[:128]
        h_part[half, 2 * pair + 1] = term[128:]

    def hidden_grads(half):
        scale = 2048.0 / count[8][0:1, 0:1]
        hidden_grad = scale * reduce_h[half].final()
        gate_f, up_f, sigmoid_gate, silu_gate = saved(half)
        g_all[2 * col + half] = (
            hidden_grad * up_f * sigmoid_gate * (1.0 + gate_f * (1.0 - sigmoid_gate))
        ).astype(BF)
        gather_g[half].start()
        u_all[2 * col + half] = (hidden_grad * silu_gate).astype(BF)
        gather_u[half].start()

    stores = []

    def store(src, dst):
        stores.append(pltpu.make_async_copy(src, dst, local_sems.at[7 + len(stores)]))
        stores[-1].start()

    def down_tile(tile):
        scale = 2048.0 / count[8][0:1, 0:1]
        at = pl.ds(tile * 448, 448)
        lhs = jnp.concatenate([h_all[slot, at, :] for slot in range(16)], axis=1)
        rhs = jnp.concatenate([w_all[slot] for slot in range(16)], axis=0)
        out_down[at, :] = (scale * jnp.dot(lhs, rhs, preferred_element_type=F32)).astype(BF)

    def weight_tile(half, acc, out, grads, tile):
        at = pl.ds(tile * 512, 512)
        lhs = jnp.concatenate([in_all[2 * c + half, at, :] for c in range(8)], axis=1)
        rhs = jnp.concatenate([grads[2 * c + half] for c in range(8)], axis=0)
        term = jnp.dot(lhs, rhs, preferred_element_type=F32)
        if half == 0:
            acc[at, :] = term
        else:
            out[at, :] = (acc[at, :] + term).astype(BF)

    first, second = reduce_h
    terms(0, 0)
    first.p0()
    terms(0, 1)
    first.p1()
    gather_h[0].g1()
    gather_h[1].rest()
    terms(0, 2)
    first.p2()
    first.t20()
    gather_i.z1()
    terms(0, 3)
    gather_h[1].g1()
    terms(1, 0)
    second.p0()
    terms(1, 1)
    second.p1()
    gather_i.f1()
    count_recv(2)
    count_send(3)
    first.s01()
    first.tm10()
    terms(1, 2)
    second.p2()
    second.t20()
    terms(1, 3)
    gather_i.rest()
    count_recv(3)
    hidden_grads(0)
    second.s01()
    second.tm10()
    gather_h[0].last()
    gather_h[1].last()
    gather_i.g1()
    gather_i.last()
    gather_g[0].z1()
    gather_u[0].z1()
    hidden_grads(1)
    down_tile(0)
    gather_g[0].f1()
    gather_u[0].f1()
    gather_g[1].z1()
    gather_u[1].z1()
    down_tile(1)
    store(out_down, grad_down)
    gather_g[0].rest()
    gather_u[0].rest()
    gather_g[1].f1()
    gather_u[1].f1()
    gather_g[0].g1()
    gather_u[0].g1()
    gather_i.from_sibling()
    loads["gw"].wait()
    loads["uw"].wait()

    class RowReduce:
        def __init__(self, half):
            self.half = half
            self.ids = [wire.new() for _ in ORDER]
            self.ring = Reduce(wire, q_part.at[half], q_got, row_m, row_p, row_z, keep=False)

        def when_owner(self, do):
            pl.when(core == self.half)(do)

        def compute(self, pair):
            slots = [
                row_of(flip(z_lo, d[1]), x + (1 - 2 * self.half) * d[0], self.half)
                for d in ORDER[2 * pair : 2 * pair + 2]
            ]
            gate_rows = jnp.concatenate([g_all[slot] for slot in slots], axis=0)
            up_rows = jnp.concatenate([u_all[slot] for slot in slots], axis=0)
            term = lax.dot_general(gate_rows, gw[...], NT, preferred_element_type=F32)
            term = term + lax.dot_general(up_rows, uw[...], NT, preferred_element_type=F32)
            q_part[self.half, 2 * pair] = term[:128].astype(BF)
            q_part[self.half, 2 * pair + 1] = term[128:].astype(BF)

            @pl.when(core != self.half)
            def _():
                for index in (2 * pair, 2 * pair + 1):
                    wire.send(
                        self.ids[index],
                        q_part.at[self.half, index],
                        q_sib.at[index],
                        sibling,
                        keep=False,
                    )

        def collect(self, pair):
            for index in (2 * pair, 2 * pair + 1):
                wire.recv(self.ids[index], q_sib.at[index])
                q_part[self.half, index] = (
                    q_part[self.half, index].astype(F32) + q_sib[index].astype(F32)
                ).astype(BF)

        def drain(self):
            @pl.when(core != self.half)
            def _():
                for index in range(8):
                    wire.copy(
                        self.ids[index],
                        q_part.at[self.half, index],
                        q_sib.at[index],
                        sibling,
                    ).wait_send()

            self.when_owner(self.ring.drain)

    def row_stage(reduce, pair):
        def do():
            reduce.collect(pair)
            if pair == 0:
                reduce.ring.p0()
            elif pair == 1:
                reduce.ring.p1()
            elif pair == 2:
                reduce.ring.p2()
                reduce.ring.t20()

        reduce.when_owner(do)

    def finish(reduce):
        def do():
            out_in[...] = reduce.ring.final().astype(BF)

        reduce.when_owner(do)

    rows0, rows1 = RowReduce(0), RowReduce(1)

    gather_g[0].last()
    gather_u[0].last()
    rows0.compute(0)
    gather_g[1].rest()
    rows0.compute(1)
    gather_u[1].rest()
    row_stage(rows0, 0)
    rows0.compute(2)
    row_stage(rows0, 1)
    rows0.compute(3)
    row_stage(rows0, 2)
    gather_g[1].g1()
    row_stage(rows0, 3)
    weight_tile(0, acc_gate, out_gate, g_all, 0)
    rows0.when_owner(rows0.ring.s01)
    rows0.when_owner(rows0.ring.tm10)
    gather_u[1].g1()
    weight_tile(0, acc_gate, out_gate, g_all, 1)
    weight_tile(0, acc_up, out_up, u_all, 0)
    weight_tile(0, acc_up, out_up, u_all, 1)
    finish(rows0)

    gather_g[1].last()
    gather_u[1].last()
    rows1.compute(0)
    rows1.compute(1)
    row_stage(rows1, 0)
    rows1.compute(2)
    row_stage(rows1, 1)
    rows1.compute(3)
    row_stage(rows1, 2)
    row_stage(rows1, 3)
    weight_tile(1, acc_gate, out_gate, g_all, 0)
    rows1.when_owner(rows1.ring.s01)
    rows1.when_owner(rows1.ring.tm10)
    weight_tile(1, acc_gate, out_gate, g_all, 1)
    store(out_gate, grad_gate)
    weight_tile(1, acc_up, out_up, u_all, 0)
    weight_tile(1, acc_up, out_up, u_all, 1)
    store(out_up, grad_up)
    finish(rows1)
    last = pltpu.make_async_copy(out_in, grad_input, local_sems.at[3])
    last.start()
    wire.drain()
    rows0.drain()
    rows1.drain()
    for copy in stores:
        copy.wait()
    last.wait()
    assert wire.count == N_MESSAGES, wire.count


def shards(
    inputs, upstream, mask_flags, levels, gate_saved, up_saved, gate_weight, up_weight, down_weight
):
    anywhere = pl.BlockSpec(memory_space=pl.ANY)
    return pl.pallas_call(
        kernel,
        out_shape=(
            jax.ShapeDtypeStruct((128, 1024), BF),
            jax.ShapeDtypeStruct((1024, 896), BF),
            jax.ShapeDtypeStruct((1024, 896), BF),
            jax.ShapeDtypeStruct((896, 1024), BF),
        ),
        in_specs=[
            pl.BlockSpec(memory_space=pltpu.SMEM),
            pl.BlockSpec(memory_space=pltpu.VMEM),
        ]
        + [anywhere] * 7,
        out_specs=(anywhere,) * 4,
        scratch_shapes=[
            pltpu.VMEM((16, 128, 1024), BF),
            pltpu.VMEM((16, 1024, 128), BF),
            pltpu.VMEM((16, 896, 128), BF),
            pltpu.VMEM((16, 128, 896), BF),
            pltpu.VMEM((16, 128, 896), BF),
            pltpu.VMEM((1024, 896), BF),
            pltpu.VMEM((1024, 896), BF),
            pltpu.VMEM((896, 1024), BF),
            pltpu.VMEM((128, 1024), BF),
            pltpu.VMEM((128, 1024), BF),
            pltpu.VMEM((256, 896), BF),
            pltpu.VMEM((256, 896), BF),
            pltpu.VMEM((2, 8, 128, 896), BF),
            pltpu.VMEM((2, 7, 128, 896), BF),
            pltpu.VMEM((2, 8, 128, 1024), BF),
            pltpu.VMEM((8, 128, 1024), BF),
            pltpu.VMEM((7, 128, 1024), BF),
            pltpu.VMEM((1024, 896), F32),
            pltpu.VMEM((1024, 896), F32),
            pltpu.VMEM((1024, 896), BF),
            pltpu.VMEM((1024, 896), BF),
            pltpu.VMEM((896, 1024), BF),
            pltpu.VMEM((128, 1024), BF),
            pltpu.VMEM((9, 8, 128), F32),
            pltpu.SemaphoreType.DMA((N_MESSAGES,)),
            pltpu.SemaphoreType.DMA((N_MESSAGES,)),
            pltpu.SemaphoreType.DMA((N_LOCAL,)),
        ],
        compiler_params=pltpu.CompilerParams(
            collective_id=0, has_side_effects=True, vmem_limit_bytes=62 * 2**20
        ),
        cost_estimate=pl.CostEstimate(
            flops=12 * 2048 * 1024 * 896, bytes_accessed=16 * 2**20, transcendentals=2 * 256 * 896
        ),
        name="swiglu_backward",
    )(
        levels,
        mask_flags.reshape(1, -1),
        inputs,
        upstream,
        gate_saved,
        up_saved,
        gate_weight,
        up_weight,
        down_weight,
    )


def solution(mesh):
    placed = (
        P("row", "col"),
        P("row", "col"),
        P("row"),
        P(),
        P("col", "row"),
        P("col", "row"),
        P("col", "row"),
        P("col", "row"),
        P("row", "col"),
    )
    return jax.shard_map(
        shards,
        mesh=mesh,
        in_specs=placed,
        out_specs=(P("row", "col"), P("col", "row"), P("col", "row"), P("row", "col")),
        check_vma=False,
    )
```

```python
import jax
import jax.numpy as jnp
from jax import lax
from jax.experimental import pallas as pl
from jax.experimental.pallas import tpu as pltpu
from jax.sharding import PartitionSpec as P

SEQ = 512
BF = jnp.bfloat16
F32 = jnp.float32
MESH = pl.DeviceIdType.MESH
NT = (((1,), (1,)), ((), ()))
ORDER = ((2, 1), (2, 0), (1, 1), (-1, 1), (1, 0), (-1, 0), (0, 1), (0, 0))


class Wire:
    def __init__(self, send_sems, recv_sems, anyone):
        self.send_sems, self.recv_sems, self.anyone = send_sems, recv_sems, anyone
        self.count = 0
        self.sent = []

    def new(self):
        self.count += 1
        return self.count - 1

    def copy(self, number, src, dst, device):
        return pltpu.make_async_remote_copy(
            src_ref=src,
            dst_ref=dst,
            send_sem=self.send_sems.at[number],
            recv_sem=self.recv_sems.at[number],
            device_id=device,
            device_id_type=MESH,
        )

    def send(self, number, src, dst, device, keep=True):
        self.copy(number, src, dst, device).start()
        if keep:
            self.sent.append((number, src, dst, device))

    def recv(self, number, dst):
        self.copy(number, dst, dst, self.anyone).wait_recv()

    def drain(self):
        for message in self.sent:
            self.copy(*message).wait_send()


class Gather:
    def __init__(
        self, wire, buf, slot, minus, plus, across, sibling=None, other_slot=None, far_z=True
    ):
        self.far_z = far_z
        self.wire, self.buf, self.slot = wire, buf, slot
        self.minus, self.plus, self.across = minus, plus, across
        self.sibling, self.other_slot = sibling, other_slot
        self.ids = {
            name: wire.new()
            for name in ("own_m", "own_p", "own_z", "z_m", "z_p", "fwd_p", "far")
        }
        self.sib_ids = {d: wire.new() for d in ORDER} if sibling is not None else {}

    def push(self, name, d, device):
        ref = self.buf.at[self.slot(d)]
        self.wire.send(self.ids[name], ref, ref, device)

    def share(self, d):
        if self.sibling is not None:
            ref = self.buf.at[self.slot(d)]
            self.wire.send(self.sib_ids[d], ref, ref, self.sibling)

    def take(self, name, d):
        self.wire.recv(self.ids[name], self.buf.at[self.slot(d)])

    def start(self):
        self.push("own_z", (0, 0), self.across)
        self.push("own_m", (0, 0), self.minus)
        self.push("own_p", (0, 0), self.plus)
        self.share((0, 0))

    def z1(self):
        self.take("own_z", (0, 1))
        self.push("z_m", (0, 1), self.minus)
        self.push("z_p", (0, 1), self.plus)
        self.share((0, 1))

    def f1(self):
        self.take("own_p", (-1, 0))
        self.push("fwd_p", (-1, 0), self.plus)
        self.share((-1, 0))

    def g1(self):
        if self.far_z:
            self.take("fwd_p", (2, 0))
            self.push("far", (2, 0), self.across)
            self.share((2, 0))
        else:
            self.take("z_m", (1, 1))
            self.push("far", (1, 1), self.minus)
            self.share((1, 1))

    def rest(self):
        self.take("own_m", (1, 0))
        self.share((1, 0))
        self.take("z_p", (-1, 1))
        self.share((-1, 1))
        if self.far_z:
            self.take("z_m", (1, 1))
            self.share((1, 1))

    def last(self):
        if not self.far_z:
            self.take("fwd_p", (2, 0))
            self.share((2, 0))
        self.take("far", (2, 1))
        self.share((2, 1))

    def sib(self):
        for d in ORDER:
            self.wire.recv(self.sib_ids[d], self.buf.at[self.other_slot(d)])


class Reduce:
    def __init__(self, wire, part, got, minus, plus, across, keep=True):
        self.wire, self.part, self.got = wire, part, got
        self.minus, self.plus, self.across, self.keep = minus, plus, across, keep
        self.ids = [wire.new() for _ in range(7)]
        self.log = []

    def push(self, index, d, device):
        src = self.part.at[ORDER.index(d)]
        message = (self.ids[index], src, self.got.at[index], device)
        self.wire.send(*message, keep=self.keep)
        self.log.append((index, d, device))

    def drain(self):
        for index, d, device in self.log:
            src = self.part.at[ORDER.index(d)]
            self.wire.copy(self.ids[index], src, self.got.at[index], device).wait_send()

    def add(self, d, *indices):
        term = self.part[ORDER.index(d)].astype(F32)
        for index in indices:
            self.wire.recv(self.ids[index], self.got.at[index])
            term = term + self.got[index].astype(F32)
        return term

    def store(self, d, term):
        self.part[ORDER.index(d)] = term.astype(BF)

    def p0(self):
        self.push(0, (2, 1), self.across)

    def p1(self):
        self.push(2, (1, 1), self.plus)
        self.push(3, (-1, 1), self.minus)

    def p2(self):
        self.push(4, (1, 0), self.plus)

    def t20(self):
        self.store((2, 0), self.add((2, 0), 0))
        self.push(1, (2, 0), self.minus)

    def tm10(self):
        self.store((-1, 0), self.add((-1, 0), 1))
        self.push(5, (-1, 0), self.minus)

    def s01(self):
        self.store((0, 1), self.add((0, 1), 2, 3))
        self.push(6, (0, 1), self.across)

    def final(self):
        return self.add((0, 0), 4, 6, 5)


N_MESSAGES = 2 * 15 + 3 * 2 * 7 + 2 * 7 + 2 * (8 + 7) + 4
N_LOCAL = 10


def kernel(
    levels,
    mask_row,
    inputs,
    upstream,
    gate_saved,
    up_saved,
    gate_weight,
    up_weight,
    down_weight,
    grad_input,
    grad_gate,
    grad_up,
    grad_down,
    w_all,
    in_all,
    h_all,
    g_all,
    u_all,
    gw,
    uw,
    dw,
    up_own,
    in_own,
    gs,
    us,
    h_part,
    h_got,
    q_part,
    q_sib,
    q_got,
    q_acc,
    acc_gate,
    acc_up,
    out_gate,
    out_up,
    out_down,
    out_in,
    count,
    send_sems,
    recv_sems,
    local_sems,
):
    row, col = lax.axis_index("row"), lax.axis_index("col")
    z_lo, x, core = row // 8, (row // 2) % 4, row % 2
    y, z_hi = col // 2, col % 2
    sign = 1 - 2 * core

    def row_of(z, x_at, k):
        return z * 8 + lax.rem(x_at + 8, 4) * 2 + k

    def col_of(y_at, z):
        return lax.rem(y_at + 8, 4) * 2 + z

    sibling = (row_of(z_lo, x, 1 - core), col)
    row_z = (row_of(1 - z_lo, x, core), col)
    row_m, row_p = (row_of(z_lo, x - sign, core), col), (row_of(z_lo, x + sign, core), col)
    col_z = (row, col_of(y, 1 - z_hi))
    col_m, col_p = (row, col_of(y - sign, z_hi)), (row, col_of(y + sign, z_hi))

    def flip(bit, d):
        return 1 - bit if d else bit

    def row_slot(d, k=core):
        return row_of(flip(z_lo, d[1]), x + sign * d[0], k)

    def col_slot(d, half):
        return 2 * col_of(y + sign * d[0], flip(z_hi, d[1])) + half

    loads = {}
    for number, (name, src, dst) in enumerate(
        (
            ("upstream", upstream, up_own),
            ("gs", gate_saved, gs),
            ("us", up_saved, us),
            ("inputs", inputs, in_own),
            ("dw", down_weight, dw),
            ("gw", gate_weight, gw),
            ("uw", up_weight, uw),
        )
    ):
        loads[name] = pltpu.make_async_copy(src, dst, local_sems.at[number])
        loads[name].start()

    barrier = pltpu.get_barrier_semaphore()
    neighbours = (sibling, row_z, row_m, row_p, col_z, col_m, col_p)
    for device in neighbours:
        pl.semaphore_signal(barrier, inc=1, device_id=device, device_id_type=MESH)

    flags = jnp.transpose(jnp.broadcast_to(mask_row[...].astype(F32), (128, 128)))
    noise = jnp.full((1, 128), levels[row * 128 // SEQ], jnp.int32).astype(F32) / 1000.0
    factor = flags / noise
    loads["upstream"].wait()
    w_all[row] = (up_own[...].astype(F32) * jnp.concatenate([factor] * 8, axis=1)).astype(BF)
    count[0] = jnp.broadcast_to(jnp.sum(flags, axis=0, keepdims=True), (8, 128))

    pl.semaphore_wait(barrier, len(neighbours))

    wire = Wire(send_sems, recv_sems, sibling)
    def row_gather(buf, far_z):
        return Gather(
            wire, buf, row_slot, row_m, row_p, row_z, sibling, lambda d: row_slot(d, 1 - core), far_z
        )

    def col_gather(buf, half):
        return Gather(wire, buf, lambda d: col_slot(d, half), col_m, col_p, col_z)

    W, I = row_gather(w_all, False), row_gather(in_all, False)
    H0, H1 = (col_gather(h_all, half) for half in range(2))
    G0, G1 = (col_gather(g_all, half) for half in range(2))
    U0, U1 = (col_gather(u_all, half) for half in range(2))

    step = 1 - 2 * lax.rem(x, 2)
    partners = (
        sibling,
        row_z,
        (row_of(z_lo, x + step, core), col),
        (row_of(z_lo, x - step, core), col),
    )
    count_ids = [wire.new() for _ in partners]

    def count_send(stage):
        wire.send(count_ids[stage], count.at[2 * stage], count.at[2 * stage + 1], partners[stage])

    def count_recv(stage):
        wire.recv(count_ids[stage], count.at[2 * stage + 1])
        count[2 * stage + 2] = count[2 * stage] + count[2 * stage + 1]

    def saved(half):
        gate_f = gs[pl.ds(half * 128, 128), :].astype(F32)
        up_f = us[pl.ds(half * 128, 128), :].astype(F32)
        sigmoid_gate = jax.nn.sigmoid(gate_f)
        return gate_f, up_f, sigmoid_gate, sigmoid_gate * gate_f

    def hidden(half, gather):
        _, up_f, _, silu_gate = saved(half)
        values = (silu_gate * up_f).astype(BF).astype(F32)
        h_all[2 * col + half] = jnp.transpose(values).astype(BF)
        gather.start()

    class ColReduce(Reduce):
        def __init__(self, half):
            self.half = half
            super().__init__(wire, h_part.at[half], h_got.at[half], col_m, col_p, col_z)

        def c(self, pair):
            ds = ORDER[2 * pair : 2 * pair + 2]
            rows = jnp.concatenate([w_all[col_slot(d, self.half)] for d in ds], axis=0)
            term = lax.dot_general(rows, dw[...], NT, preferred_element_type=F32).astype(BF)
            h_part[self.half, 2 * pair] = term[:128]
            h_part[self.half, 2 * pair + 1] = term[128:]
            if pair < 3:
                (self.p0, self.p1, self.p2)[pair]()

    def hidden_grads(half, reduce, gather):
        scale = 2048.0 / count[8][0:1, 0:1]
        hidden_grad = scale * reduce.final()
        gate_f, up_f, sigmoid_gate, silu_gate = saved(half)
        g_all[2 * col + half] = (
            hidden_grad * up_f * sigmoid_gate * (1.0 + gate_f * (1.0 - sigmoid_gate))
        ).astype(BF)
        gather.start()
        u_all[2 * col + half] = (hidden_grad * silu_gate).astype(BF)

    stores = []

    def store(src, dst):
        stores.append(pltpu.make_async_copy(src, dst, local_sems.at[7 + len(stores)]))
        stores[-1].start()

    def down(tile):
        scale = 2048.0 / count[8][0:1, 0:1]
        at = pl.ds(tile * 224, 224)
        lhs = jnp.concatenate([h_all[slot, at, :] for slot in range(16)], axis=1)
        rhs = jnp.concatenate([w_all[slot] for slot in range(16)], axis=0)
        out_down[at, :] = (scale * jnp.dot(lhs, rhs, preferred_element_type=F32)).astype(BF)
        if tile == 3:
            store(out_down, grad_down)

    def weight(half, tile, grads, acc, out, result):
        at = pl.ds(tile * 512, 512)
        lhs = jnp.concatenate([in_all[2 * c + half, at, :] for c in range(8)], axis=1)
        rhs = jnp.concatenate([grads[2 * c + half] for c in range(8)], axis=0)
        term = jnp.dot(lhs, rhs, preferred_element_type=F32)
        if half == 0:
            acc[at, :] = term
        else:
            out[at, :] = (acc[at, :] + term).astype(BF)
            if tile == 1:
                store(out, result)

    class RowReduce:
        def __init__(self, half):
            self.half = half
            self.ids = [wire.new() for _ in ORDER]
            self.ring = Reduce(wire, q_part.at[half], q_got, row_m, row_p, row_z, keep=False)

        def when_owner(self, do):
            pl.when(core == self.half)(do)

        def rows(self, grads, pair):
            slots = [
                row_of(flip(z_lo, d[1]), x + (1 - 2 * self.half) * d[0], self.half)
                for d in ORDER[2 * pair : 2 * pair + 2]
            ]
            return jnp.concatenate([grads[slot] for slot in slots], axis=0)

        def a(self, pair):
            q_acc[pair] = lax.dot_general(
                self.rows(g_all, pair), gw[...], NT, preferred_element_type=F32
            )

        def c(self, pair):
            term = q_acc[pair] + lax.dot_general(
                self.rows(u_all, pair), uw[...], NT, preferred_element_type=F32
            )
            q_part[self.half, 2 * pair] = term[:128].astype(BF)
            q_part[self.half, 2 * pair + 1] = term[128:].astype(BF)

            @pl.when(core != self.half)
            def _():
                for index in (2 * pair, 2 * pair + 1):
                    wire.send(
                        self.ids[index],
                        q_part.at[self.half, index],
                        q_sib.at[index],
                        sibling,
                        keep=False,
                    )

        def k(self, pair):
            def do():
                for index in (2 * pair, 2 * pair + 1):
                    wire.recv(self.ids[index], q_sib.at[index])
                    q_part[self.half, index] = (
                        q_part[self.half, index].astype(F32) + q_sib[index].astype(F32)
                    ).astype(BF)
                if pair < 3:
                    (self.ring.p0, self.ring.p1, self.ring.p2)[pair]()

            self.when_owner(do)

        def t20(self):
            self.when_owner(self.ring.t20)

        def tm10(self):
            self.when_owner(self.ring.tm10)

        def s01(self):
            self.when_owner(self.ring.s01)

        def fin(self):
            def do():
                out_in[...] = self.ring.final().astype(BF)

            self.when_owner(do)

        def drain(self):
            @pl.when(core != self.half)
            def _():
                for index in range(8):
                    wire.copy(
                        self.ids[index],
                        q_part.at[self.half, index],
                        q_sib.at[index],
                        sibling,
                    ).wait_send()

            self.when_owner(self.ring.drain)

    R0, R1 = ColReduce(0), ColReduce(1)
    Q0, Q1 = RowReduce(0), RowReduce(1)

    W.start()
    count_send(0)
    loads["gs"].wait()
    loads["us"].wait()
    hidden(0, H0)
    hidden(1, H1)
    loads["inputs"].wait()
    in_all[row] = jnp.transpose(in_own[...].astype(F32)).astype(BF)
    W.z1()
    count_recv(0)
    count_send(1)
    W.f1()
    H0.f1()
    W.g1()
    H0.z1()
    H1.f1()
    W.rest()
    H0.g1()
    H1.z1()
    W.last()
    count_recv(1)
    count_send(2)
    H0.rest()
    H0.last()
    W.sib()
    H1.g1()
    loads["dw"].wait()
    R0.c(0)
    R0.c(1)
    count_recv(2)
    count_send(3)
    R0.c(2)
    R0.c(3)
    R1.c(0)
    H1.rest()
    I.start()
    R1.c(1)
    R1.c(2)
    H1.last()
    R1.c(3)
    count_recv(3)
    down(0)
    down(1)
    R0.s01()
    down(2)
    R0.t20()
    I.f1()
    down(3)
    R1.t20()
    R1.s01()
    I.z1()
    R0.tm10()
    R1.tm10()
    I.g1()
    hidden_grads(0, R0, G0)
    U0.start()
    I.rest()
    hidden_grads(1, R1, G1)
    U1.start()
    I.last()
    G0.f1()
    I.sib()
    G0.z1()
    U0.f1()
    U0.z1()
    G1.f1()
    G1.z1()
    U1.f1()
    U1.z1()
    G0.g1()
    G0.rest()
    G0.last()
    weight(0, 0, g_all, acc_gate, out_gate, grad_gate)
    U0.g1()
    weight(0, 1, g_all, acc_gate, out_gate, grad_gate)
    loads["gw"].wait()
    loads["uw"].wait()
    Q0.a(0)
    Q0.a(1)
    Q0.a(2)
    Q0.a(3)
    U0.rest()
    U0.last()
    Q0.c(0)
    G1.g1()
    Q0.c(1)
    Q0.c(2)
    Q0.c(3)
    weight(0, 0, u_all, acc_up, out_up, grad_up)
    Q0.k(0)
    Q0.k(1)
    weight(0, 1, u_all, acc_up, out_up, grad_up)
    Q0.k(2)
    Q0.k(3)
    G1.rest()
    G1.last()
    Q1.a(0)
    U1.g1()
    Q1.a(1)
    Q1.a(2)
    Q0.s01()
    Q1.a(3)
    Q0.t20()
    weight(1, 0, g_all, acc_gate, out_gate, grad_gate)
    weight(1, 1, g_all, acc_gate, out_gate, grad_gate)
    U1.rest()
    U1.last()
    Q1.c(0)
    Q0.tm10()
    Q1.c(1)
    Q1.c(2)
    Q1.c(3)
    Q1.k(0)
    weight(1, 0, u_all, acc_up, out_up, grad_up)
    Q1.k(1)
    Q0.fin()
    Q1.k(2)
    weight(1, 1, u_all, acc_up, out_up, grad_up)
    Q1.k(3)
    Q1.t20()
    Q1.s01()
    Q1.tm10()
    Q1.fin()
    last = pltpu.make_async_copy(out_in, grad_input, local_sems.at[3])
    last.start()
    wire.drain()
    Q0.drain()
    Q1.drain()
    for copy in stores:
        copy.wait()
    last.wait()
    assert wire.count == N_MESSAGES, wire.count


def move(*refs):
    sources, results, held, sems = refs[:4], refs[4:8], refs[8:12], refs[12]
    pieces = []
    for array in range(4):
        rows = sources[array].shape[0] // 2
        for part in range(2):
            at = pl.ds(part * rows, rows)
            number = 2 * (2 * array + part)
            load = pltpu.make_async_copy(
                sources[array].at[at], held[array].at[at], sems.at[number]
            )
            save = pltpu.make_async_copy(
                held[array].at[at], results[array].at[at], sems.at[number + 1]
            )
            pieces.append((load, save))
    for load, _ in pieces:
        load.start()
    for load, save in pieces:
        load.wait()
        save.start()
    for _, save in pieces:
        save.wait()


def shards(
    inputs, upstream, mask_flags, levels, gate_saved, up_saved, gate_weight, up_weight, down_weight
):
    anywhere = pl.BlockSpec(memory_space=pl.ANY)
    results = (
        jax.ShapeDtypeStruct((128, 1024), BF),
        jax.ShapeDtypeStruct((1024, 896), BF),
        jax.ShapeDtypeStruct((1024, 896), BF),
        jax.ShapeDtypeStruct((896, 1024), BF),
    )
    grads = pl.pallas_call(
        kernel,
        out_shape=results,
        in_specs=[
            pl.BlockSpec(memory_space=pltpu.SMEM),
            pl.BlockSpec(memory_space=pltpu.VMEM),
        ]
        + [anywhere] * 7,
        out_specs=(anywhere,) * 4,
        scratch_shapes=[
            pltpu.VMEM((16, 128, 1024), BF),
            pltpu.VMEM((16, 1024, 128), BF),
            pltpu.VMEM((16, 896, 128), BF),
            pltpu.VMEM((16, 128, 896), BF),
            pltpu.VMEM((16, 128, 896), BF),
            pltpu.VMEM((1024, 896), BF),
            pltpu.VMEM((1024, 896), BF),
            pltpu.VMEM((896, 1024), BF),
            pltpu.VMEM((128, 1024), BF),
            pltpu.VMEM((128, 1024), BF),
            pltpu.VMEM((256, 896), BF),
            pltpu.VMEM((256, 896), BF),
            pltpu.VMEM((2, 8, 128, 896), BF),
            pltpu.VMEM((2, 7, 128, 896), BF),
            pltpu.VMEM((2, 8, 128, 1024), BF),
            pltpu.VMEM((8, 128, 1024), BF),
            pltpu.VMEM((7, 128, 1024), BF),
            pltpu.VMEM((4, 256, 1024), F32),
            pltpu.VMEM((1024, 896), F32),
            pltpu.VMEM((1024, 896), F32),
            pltpu.VMEM((1024, 896), BF),
            pltpu.VMEM((1024, 896), BF),
            pltpu.VMEM((896, 1024), BF),
            pltpu.VMEM((128, 1024), BF),
            pltpu.VMEM((9, 8, 128), F32),
            pltpu.SemaphoreType.DMA((N_MESSAGES,)),
            pltpu.SemaphoreType.DMA((N_MESSAGES,)),
            pltpu.SemaphoreType.DMA((N_LOCAL,)),
        ],
        compiler_params=pltpu.CompilerParams(
            collective_id=0, has_side_effects=True, vmem_limit_bytes=62 * 2**20
        ),
        cost_estimate=pl.CostEstimate(
            flops=12 * 2048 * 1024 * 896, bytes_accessed=16 * 2**20, transcendentals=2 * 256 * 896
        ),
        name="swiglu_backward",
    )(
        levels,
        mask_flags.reshape(1, -1),
        inputs,
        upstream,
        gate_saved,
        up_saved,
        gate_weight,
        up_weight,
        down_weight,
    )
    return pl.pallas_call(
        move,
        out_shape=results,
        in_specs=[anywhere] * 4,
        out_specs=(anywhere,) * 4,
        scratch_shapes=[pltpu.VMEM(result.shape, BF) for result in results]
        + [pltpu.SemaphoreType.DMA((16,))],
        compiler_params=pltpu.CompilerParams(vmem_limit_bytes=62 * 2**20),
        name="move_results",
    )(*grads)


def solution(mesh):
    placed = (
        P("row", "col"),
        P("row", "col"),
        P("row"),
        P(),
        P("col", "row"),
        P("col", "row"),
        P("col", "row"),
        P("col", "row"),
        P("row", "col"),
    )
    return jax.shard_map(
        shards,
        mesh=mesh,
        in_specs=placed,
        out_specs=(P("row", "col"), P("col", "row"), P("col", "row"), P("row", "col")),
        check_vma=False,
    )
```

```python
import jax
import jax.numpy as jnp
from jax import lax
from jax.experimental import pallas as pl
from jax.experimental.pallas import tpu as pltpu
from jax.sharding import PartitionSpec as P

SEQ = 512
BF = jnp.bfloat16
F32 = jnp.float32
MESH = pl.DeviceIdType.MESH
NT = (((1,), (1,)), ((), ()))
MIRROR = (0, 1, 3, 2, 5, 4, 6, 7)
ORDER = ((2, 1), (2, 0), (1, 1), (-1, 1), (1, 0), (-1, 0), (0, 1), (0, 0))


class Wire:
    def __init__(self, send_sems, recv_sems, anyone):
        self.send_sems, self.recv_sems, self.anyone = send_sems, recv_sems, anyone
        self.count = 0
        self.sent = []

    def new(self):
        self.count += 1
        return self.count - 1

    def copy(self, number, src, dst, device):
        return pltpu.make_async_remote_copy(
            src_ref=src,
            dst_ref=dst,
            send_sem=self.send_sems.at[number],
            recv_sem=self.recv_sems.at[number],
            device_id=device,
            device_id_type=MESH,
        )

    def send(self, number, src, dst, device):
        self.copy(number, src, dst, device).start()
        self.sent.append((number, src, dst, device))

    def recv(self, number, dst):
        self.copy(number, dst, dst, self.anyone).wait_recv()

    def drain(self, numbers=None):
        chosen = [m for m in self.sent if numbers is None or m[0] in numbers]
        self.sent = [m for m in self.sent if m not in chosen]
        for message in chosen:
            self.copy(*message).wait_send()


class Gather:
    def __init__(
        self, wire, at, minus, plus, across, sibling=None, other_at=None, far_z=True
    ):
        self.far_z = far_z
        self.wire, self.at = wire, at
        self.minus, self.plus, self.across = minus, plus, across
        self.sibling, self.other_at = sibling, other_at
        self.ids = {
            name: wire.new()
            for name in ("own_m", "own_p", "own_z", "z_m", "z_p", "fwd_p", "far")
        }
        self.sib_ids = {d: wire.new() for d in ORDER} if sibling is not None else {}

    def push(self, name, d, device):
        ref = self.at(d)
        self.wire.send(self.ids[name], ref, ref, device)

    def share(self, d):
        if self.sibling is not None:
            ref = self.at(d)
            self.wire.send(self.sib_ids[d], ref, ref, self.sibling)

    def take(self, name, d):
        self.wire.recv(self.ids[name], self.at(d))

    def start(self):
        self.push("own_z", (0, 0), self.across)
        self.push("own_m", (0, 0), self.minus)
        self.push("own_p", (0, 0), self.plus)
        self.share((0, 0))

    def z1(self):
        self.take("own_z", (0, 1))
        self.push("z_m", (0, 1), self.minus)
        self.push("z_p", (0, 1), self.plus)
        self.share((0, 1))

    def f1(self):
        self.take("own_p", (-1, 0))
        self.push("fwd_p", (-1, 0), self.plus)
        self.share((-1, 0))

    def g1(self):
        if self.far_z:
            self.take("fwd_p", (2, 0))
            self.push("far", (2, 0), self.across)
            self.share((2, 0))
        else:
            self.take("z_m", (1, 1))
            self.push("far", (1, 1), self.minus)
            self.share((1, 1))

    def rest(self):
        self.take("own_m", (1, 0))
        self.share((1, 0))
        self.take("z_p", (-1, 1))
        self.share((-1, 1))
        if self.far_z:
            self.take("z_m", (1, 1))
            self.share((1, 1))

    def last(self):
        if not self.far_z:
            self.take("fwd_p", (2, 0))
            self.share((2, 0))
        self.take("far", (2, 1))
        self.share((2, 1))

    def sib(self):
        for d in ORDER:
            self.wire.recv(self.sib_ids[d], self.other_at(d))


class Reduce:
    def __init__(self, wire, part, got, minus, plus, across):
        self.wire, self.part, self.got = wire, part, got
        self.minus, self.plus, self.across = minus, plus, across
        self.ids = [wire.new() for _ in range(7)]

    def push(self, index, d, device):
        self.wire.send(self.ids[index], self.part(ORDER.index(d)), self.got.at[index], device)

    def add(self, d, *indices):
        term = self.part(ORDER.index(d))[...].astype(F32)
        for index in indices:
            self.wire.recv(self.ids[index], self.got.at[index])
            term = term + self.got[index].astype(F32)
        return term

    def store(self, d, term):
        self.part(ORDER.index(d))[...] = term.astype(BF)

    def p0(self):
        self.push(0, (2, 1), self.across)

    def p1(self):
        self.push(2, (1, 1), self.plus)
        self.push(3, (-1, 1), self.minus)

    def p2(self):
        self.push(4, (1, 0), self.plus)

    def t20(self):
        self.store((2, 0), self.add((2, 0), 0))
        self.push(1, (2, 0), self.minus)

    def tm10(self):
        self.store((-1, 0), self.add((-1, 0), 1))
        self.push(5, (-1, 0), self.minus)

    def s01(self):
        self.store((0, 1), self.add((0, 1), 2, 3))
        self.push(6, (0, 1), self.across)

    def final(self):
        return self.add((0, 0), 4, 6, 5)


N_MESSAGES = 3 * 15 + 3 * 2 * 7 + 2 * 7 + 2 * (8 + 7) + 4
N_LOCAL = 10


def kernel(
    levels,
    mask_row,
    inputs,
    upstream,
    gate_saved,
    up_saved,
    gate_weight,
    up_weight,
    down_weight,
    grad_input,
    grad_gate,
    grad_up,
    grad_down,
    w_all,
    in_all,
    h_all,
    g_all,
    u_all,
    gw,
    uw,
    dw,
    up_own,
    in_own,
    gs,
    us,
    h_part,
    h_got,
    q_part,
    q_sib,
    q_got,
    q_acc,
    acc_down,
    acc_gate,
    acc_up,
    out_gate,
    out_up,
    out_down,
    out_in,
    count,
    send_sems,
    recv_sems,
    local_sems,
):
    row, col = lax.axis_index("row"), lax.axis_index("col")
    z_lo, x, core = row // 8, (row // 2) % 4, row % 2
    y, z_hi = col // 2, col % 2
    sign = 1 - 2 * core

    def row_of(z, x_at, k):
        return z * 8 + lax.rem(x_at + 8, 4) * 2 + k

    def col_of(y_at, z):
        return lax.rem(y_at + 8, 4) * 2 + z

    sibling = (row_of(z_lo, x, 1 - core), col)
    row_z = (row_of(1 - z_lo, x, core), col)
    row_m, row_p = (row_of(z_lo, x - sign, core), col), (row_of(z_lo, x + sign, core), col)
    col_z = (row, col_of(y, 1 - z_hi))
    col_m, col_p = (row, col_of(y - sign, z_hi)), (row, col_of(y + sign, z_hi))

    def flip(bit, d):
        return 1 - bit if d else bit

    def chip_at(d):
        return flip(z_lo, d[1]) * 4 + lax.rem(x + sign * d[0] + 8, 4)

    def row_slot(d, k=core):
        return 2 * chip_at(d) + k

    def col_at(d):
        return col_of(y + sign * d[0], flip(z_hi, d[1]))

    loads = {}
    for number, (name, src, dst) in enumerate(
        (
            ("upstream", upstream, up_own),
            ("gs", gate_saved, gs),
            ("us", up_saved, us),
            ("inputs", inputs, in_own),
            ("dw", down_weight, dw),
            ("gw", gate_weight, gw),
            ("uw", up_weight, uw),
        )
    ):
        loads[name] = pltpu.make_async_copy(src, dst, local_sems.at[number])
        loads[name].start()

    barrier = pltpu.get_barrier_semaphore()
    neighbours = (sibling, row_z, row_m, row_p, col_z, col_m, col_p)
    for device in neighbours:
        pl.semaphore_signal(barrier, inc=1, device_id=device, device_id_type=MESH)

    flags = jnp.transpose(jnp.broadcast_to(mask_row[...].astype(F32), (128, 128)))
    noise = jnp.full((1, 128), levels[row * 128 // SEQ], jnp.int32).astype(F32) / 1000.0
    factor = flags / noise
    loads["upstream"].wait()
    w_all[row] = (up_own[...].astype(F32) * jnp.concatenate([factor] * 8, axis=1)).astype(BF)
    count[0] = jnp.broadcast_to(jnp.sum(flags, axis=0, keepdims=True), (8, 128))

    pl.semaphore_wait(barrier, len(neighbours))

    wire = Wire(send_sems, recv_sems, sibling)
    def row_gather(view, far_z):
        return Gather(
            wire,
            lambda d: view(row_slot(d)),
            row_m,
            row_p,
            row_z,
            sibling,
            lambda d: view(row_slot(d, 1 - core)),
            far_z,
        )

    def col_gather(buf, half, far_z=True):
        def at(d):
            return buf.at[2 * col_at(d) + half]

        return Gather(wire, at, col_m, col_p, col_z, far_z=far_z)

    W0 = row_gather(lambda slot: w_all.at[slot, pl.ds(0, 64)], False)
    W1 = row_gather(lambda slot: w_all.at[slot, pl.ds(64, 64)], False)
    I = row_gather(lambda slot: in_all.at[slot], False)
    H0, H1 = col_gather(h_all, 0), col_gather(h_all, 1, False)
    G0, G1 = (col_gather(g_all, half) for half in range(2))
    U0, U1 = (col_gather(u_all, half) for half in range(2))

    step = 1 - 2 * lax.rem(x, 2)
    partners = (
        sibling,
        row_z,
        (row_of(z_lo, x + step, core), col),
        (row_of(z_lo, x - step, core), col),
    )
    count_ids = [wire.new() for _ in partners]

    def count_send(stage):
        wire.send(count_ids[stage], count.at[2 * stage], count.at[2 * stage + 1], partners[stage])

    def count_recv(stage):
        wire.recv(count_ids[stage], count.at[2 * stage + 1])
        count[2 * stage + 2] = count[2 * stage] + count[2 * stage + 1]

    def saved(parts):
        gate_f = jnp.concatenate([gs[at, :] for at in parts], axis=0).astype(F32)
        up_f = jnp.concatenate([us[at, :] for at in parts], axis=0).astype(F32)
        sigmoid_gate = jax.nn.sigmoid(gate_f)
        return gate_f, up_f, sigmoid_gate, sigmoid_gate * gate_f

    def hidden(half):
        _, up_f, _, silu_gate = saved([pl.ds(half * 128, 128)])
        values = (silu_gate * up_f).astype(BF).astype(F32)
        h_all[2 * col + half] = jnp.transpose(values).astype(BF)

    class ColReduce(Reduce):
        def __init__(self, half):
            self.half = half
            super().__init__(
                wire, lambda index: h_part.at[half, index], h_got.at[half], col_m, col_p, col_z
            )

        def c(self, pair):
            ds = ORDER[2 * pair : 2 * pair + 2]
            at = pl.ds(64 * self.half, 64)
            rows = jnp.concatenate(
                [w_all[2 * col_at(d) + k, at, :] for d in ds for k in range(2)], axis=0
            )
            term = lax.dot_general(rows, dw[...], NT, preferred_element_type=F32).astype(BF)
            h_part[self.half, 2 * pair] = term[:128]
            h_part[self.half, 2 * pair + 1] = term[128:]
            if pair < 3:
                (self.p0, self.p1, self.p2)[pair]()

    def hidden_grads(half, reduce, gather):
        scale = 2048.0 / count[8][0:1, 0:1]
        hidden_grad = scale * reduce.final()
        gate_f, up_f, sigmoid_gate, silu_gate = saved(
            [pl.ds(128 * k + 64 * half, 64) for k in range(2)]
        )
        g_all[2 * col + half] = (
            hidden_grad * up_f * sigmoid_gate * (1.0 + gate_f * (1.0 - sigmoid_gate))
        ).astype(BF)
        gather.start()
        u_all[2 * col + half] = (hidden_grad * silu_gate).astype(BF)

    stores = []

    def store(src, dst):
        stores.append(pltpu.make_async_copy(src, dst, local_sems.at[7 + len(stores)]))
        stores[-1].start()

    def down(half, tile):
        at = pl.ds(tile * 224, 224)
        lhs = jnp.concatenate([h_all[2 * c + half, at, :] for c in range(8)], axis=1)
        rhs = jnp.concatenate([w_all[2 * c + half] for c in range(8)], axis=0)
        term = jnp.dot(lhs, rhs, preferred_element_type=F32)
        if half == 0:
            acc_down[at, :] = term
        else:
            scale = 2048.0 / count[8][0:1, 0:1]
            out_down[at, :] = (scale * (acc_down[at, :] + term)).astype(BF)
            if tile == 3:
                store(out_down, grad_down)

    def regroup():
        wire.drain(list(I.ids.values()) + list(I.sib_ids.values()))
        for c in range(8):
            first, second = in_all[2 * c], in_all[2 * c + 1]
            in_all[2 * c] = jnp.concatenate([first[:, :64], second[:, :64]], axis=1)
            in_all[2 * c + 1] = jnp.concatenate([first[:, 64:], second[:, 64:]], axis=1)

    def weight(half, tile, grads, acc, out, result):
        at = pl.ds(tile * 256, 256)
        lhs = jnp.concatenate([in_all[2 * c + half, at, :] for c in range(8)], axis=1)
        rhs = jnp.concatenate([grads[2 * c + half] for c in range(8)], axis=0)
        term = jnp.dot(lhs, rhs, preferred_element_type=F32)
        if half == 0:
            acc[at, :] = term
        else:
            out[at, :] = (acc[at, :] + term).astype(BF)
            if tile == 3:
                store(out, result)

    class RowReduce(Reduce):
        def __init__(self, half):
            self.half = half
            self.sib_ids = [wire.new() for _ in ORDER]
            super().__init__(
                wire,
                lambda index: q_part.at[half, index, core],
                q_got.at[half],
                row_m,
                row_p,
                row_z,
            )

        def rows(self, grads, pair):
            slots = [2 * chip_at(d) + self.half for d in ORDER[2 * pair : 2 * pair + 2]]
            return jnp.concatenate([grads[slot] for slot in slots], axis=0)

        def a(self, pair):
            q_acc[pair] = lax.dot_general(
                self.rows(g_all, pair), gw[...], NT, preferred_element_type=F32
            )

        def c(self, pair):
            term = q_acc[pair] + lax.dot_general(
                self.rows(u_all, pair), uw[...], NT, preferred_element_type=F32
            )
            for part in range(4):
                q_part[self.half, 2 * pair + part // 2, part % 2] = term[
                    64 * part : 64 * part + 64
                ].astype(BF)
            for index in (2 * pair, 2 * pair + 1):
                there = MIRROR[index]
                wire.send(
                    self.sib_ids[there],
                    q_part.at[self.half, index, 1 - core],
                    q_sib.at[self.half, there],
                    sibling,
                )

        def k(self, pair):
            for index in (2 * pair, 2 * pair + 1):
                wire.recv(self.sib_ids[index], q_sib.at[self.half, index])
                own = self.part(index)
                own[...] = (
                    own[...].astype(F32) + q_sib[self.half, index].astype(F32)
                ).astype(BF)
            if pair < 3:
                (self.p0, self.p1, self.p2)[pair]()

        def fin(self):
            out_in[pl.ds(64 * self.half, 64), :] = self.final().astype(BF)

    R0, R1 = ColReduce(0), ColReduce(1)
    Q0, Q1 = RowReduce(0), RowReduce(1)

    W0.start()
    count_send(0)
    loads["inputs"].wait()
    in_all[row] = jnp.transpose(in_own[...].astype(F32)).astype(BF)
    loads["gs"].wait()
    loads["us"].wait()
    hidden(1)
    hidden(0)
    H0.start()
    W0.z1()
    count_recv(0)
    count_send(1)
    W0.f1()
    W0.g1()
    W1.start()
    W0.rest()
    H0.z1()
    H0.f1()
    W0.last()
    count_recv(1)
    count_send(2)
    W1.z1()
    W0.sib()
    W1.f1()
    loads["dw"].wait()
    R0.c(0)
    R0.c(1)
    count_recv(2)
    count_send(3)
    W1.g1()
    R0.c(2)
    W1.rest()
    H0.rest()
    R0.c(3)
    H0.g1()
    W1.last()
    R0.t20()
    W1.sib()
    R1.c(0)
    R1.c(1)
    R1.c(2)
    R1.c(3)
    R0.s01()
    H0.last()
    down(0, 0)
    down(0, 1)
    R0.tm10()
    I.start()
    down(0, 2)
    down(0, 3)
    R1.t20()
    R1.s01()
    I.f1()
    count_recv(3)
    hidden_grads(0, R0, G0)
    R1.tm10()
    I.z1()
    G0.f1()
    U0.start()
    I.g1()
    hidden_grads(1, R1, G1)
    U1.start()
    I.rest()
    G0.g1()
    G0.z1()
    I.last()
    I.sib()
    regroup()
    U0.f1()
    U0.z1()
    G1.f1()
    G1.z1()
    U1.f1()
    U1.z1()
    H1.start()
    G0.rest()
    G0.last()
    loads["gw"].wait()
    loads["uw"].wait()
    Q0.a(0)
    Q0.a(1)
    Q0.a(2)
    U0.g1()
    Q0.a(3)
    weight(0, 0, g_all, acc_gate, out_gate, grad_gate)
    weight(0, 1, g_all, acc_gate, out_gate, grad_gate)
    weight(0, 2, g_all, acc_gate, out_gate, grad_gate)
    H1.z1()
    weight(0, 3, g_all, acc_gate, out_gate, grad_gate)
    U0.rest()
    G1.g1()
    U0.last()
    Q0.c(0)
    Q0.c(1)
    Q0.c(2)
    Q0.c(3)
    Q0.k(0)
    weight(0, 0, u_all, acc_up, out_up, grad_up)
    Q0.k(1)
    Q0.k(2)
    G1.rest()
    weight(0, 1, u_all, acc_up, out_up, grad_up)
    Q0.k(3)
    weight(0, 2, u_all, acc_up, out_up, grad_up)
    G1.last()
    weight(1, 0, g_all, acc_gate, out_gate, grad_gate)
    U1.g1()
    weight(1, 1, g_all, acc_gate, out_gate, grad_gate)
    weight(1, 2, g_all, acc_gate, out_gate, grad_gate)
    Q0.t20()
    weight(1, 3, g_all, acc_gate, out_gate, grad_gate)
    Q1.a(0)
    weight(0, 3, u_all, acc_up, out_up, grad_up)
    Q1.a(1)
    U1.rest()
    Q0.tm10()
    Q1.a(2)
    Q1.a(3)
    U1.last()
    Q1.c(0)
    Q1.c(1)
    Q1.c(2)
    Q1.c(3)
    Q1.k(0)
    H1.f1()
    Q0.s01()
    Q1.k(1)
    weight(1, 0, u_all, acc_up, out_up, grad_up)
    Q1.k(2)
    Q1.k(3)
    H1.g1()
    weight(1, 1, u_all, acc_up, out_up, grad_up)
    weight(1, 2, u_all, acc_up, out_up, grad_up)
    weight(1, 3, u_all, acc_up, out_up, grad_up)
    Q1.t20()
    H1.rest()
    Q1.s01()
    Q0.fin()
    Q1.tm10()
    H1.last()
    down(1, 0)
    down(1, 1)
    down(1, 2)
    Q1.fin()
    down(1, 3)
    last = pltpu.make_async_copy(out_in, grad_input, local_sems.at[3])
    last.start()
    wire.drain()
    for copy in stores:
        copy.wait()
    last.wait()
    assert wire.count == N_MESSAGES, wire.count


def move(*refs):
    sources, results, held, sems = refs[:4], refs[4:8], refs[8:12], refs[12]
    pieces = []
    for array in range(4):
        rows = sources[array].shape[0] // 2
        for part in range(2):
            at = pl.ds(part * rows, rows)
            number = 2 * (2 * array + part)
            load = pltpu.make_async_copy(
                sources[array].at[at], held[array].at[at], sems.at[number]
            )
            save = pltpu.make_async_copy(
                held[array].at[at], results[array].at[at], sems.at[number + 1]
            )
            pieces.append((load, save))
    for load, _ in pieces:
        load.start()
    for load, save in pieces:
        load.wait()
        save.start()
    for _, save in pieces:
        save.wait()


def shards(
    inputs, upstream, mask_flags, levels, gate_saved, up_saved, gate_weight, up_weight, down_weight
):
    anywhere = pl.BlockSpec(memory_space=pl.ANY)
    results = (
        jax.ShapeDtypeStruct((128, 1024), BF),
        jax.ShapeDtypeStruct((1024, 896), BF),
        jax.ShapeDtypeStruct((1024, 896), BF),
        jax.ShapeDtypeStruct((896, 1024), BF),
    )
    grads = pl.pallas_call(
        kernel,
        out_shape=results,
        in_specs=[
            pl.BlockSpec(memory_space=pltpu.SMEM),
            pl.BlockSpec(memory_space=pltpu.VMEM),
        ]
        + [anywhere] * 7,
        out_specs=(anywhere,) * 4,
        scratch_shapes=[
            pltpu.VMEM((16, 128, 1024), BF),
            pltpu.VMEM((16, 1024, 128), BF),
            pltpu.VMEM((16, 896, 128), BF),
            pltpu.VMEM((16, 128, 896), BF),
            pltpu.VMEM((16, 128, 896), BF),
            pltpu.VMEM((1024, 896), BF),
            pltpu.VMEM((1024, 896), BF),
            pltpu.VMEM((896, 1024), BF),
            pltpu.VMEM((128, 1024), BF),
            pltpu.VMEM((128, 1024), BF),
            pltpu.VMEM((256, 896), BF),
            pltpu.VMEM((256, 896), BF),
            pltpu.VMEM((2, 8, 128, 896), BF),
            pltpu.VMEM((2, 7, 128, 896), BF),
            pltpu.VMEM((2, 8, 2, 64, 1024), BF),
            pltpu.VMEM((2, 8, 64, 1024), BF),
            pltpu.VMEM((2, 7, 64, 1024), BF),
            pltpu.VMEM((4, 256, 1024), F32),
            pltpu.VMEM((896, 1024), F32),
            pltpu.VMEM((1024, 896), F32),
            pltpu.VMEM((1024, 896), F32),
            pltpu.VMEM((1024, 896), BF),
            pltpu.VMEM((1024, 896), BF),
            pltpu.VMEM((896, 1024), BF),
            pltpu.VMEM((128, 1024), BF),
            pltpu.VMEM((9, 8, 128), F32),
            pltpu.SemaphoreType.DMA((N_MESSAGES,)),
            pltpu.SemaphoreType.DMA((N_MESSAGES,)),
            pltpu.SemaphoreType.DMA((N_LOCAL,)),
        ],
        compiler_params=pltpu.CompilerParams(
            collective_id=0, has_side_effects=True, vmem_limit_bytes=62 * 2**20
        ),
        cost_estimate=pl.CostEstimate(
            flops=12 * 2048 * 1024 * 896, bytes_accessed=16 * 2**20, transcendentals=2 * 256 * 896
        ),
        name="swiglu_backward",
    )(
        levels,
        mask_flags.reshape(1, -1),
        inputs,
        upstream,
        gate_saved,
        up_saved,
        gate_weight,
        up_weight,
        down_weight,
    )
    return pl.pallas_call(
        move,
        out_shape=results,
        in_specs=[anywhere] * 4,
        out_specs=(anywhere,) * 4,
        scratch_shapes=[pltpu.VMEM(result.shape, BF) for result in results]
        + [pltpu.SemaphoreType.DMA((16,))],
        compiler_params=pltpu.CompilerParams(vmem_limit_bytes=62 * 2**20),
        name="move_results",
    )(*grads)


def solution(mesh):
    placed = (
        P("row", "col"),
        P("row", "col"),
        P("row"),
        P(),
        P("col", "row"),
        P("col", "row"),
        P("col", "row"),
        P("col", "row"),
        P("row", "col"),
    )
    return jax.shard_map(
        shards,
        mesh=mesh,
        in_specs=placed,
        out_specs=(P("row", "col"), P("col", "row"), P("col", "row"), P("row", "col")),
        check_vma=False,
    )
```

```python
import jax
import jax.numpy as jnp
from jax import lax
from jax.experimental import pallas as pl
from jax.experimental.pallas import tpu as pltpu
from jax.sharding import PartitionSpec as P

SEQ = 512
BF = jnp.bfloat16
F32 = jnp.float32
MESH = pl.DeviceIdType.MESH
NT = (((1,), (1,)), ((), ()))
MIRROR = (0, 1, 3, 2, 5, 4, 6, 7)
ORDER = ((2, 1), (2, 0), (1, 1), (-1, 1), (1, 0), (-1, 0), (0, 1), (0, 0))


class Wire:
    def __init__(self, send_sems, recv_sems, anyone):
        self.send_sems, self.recv_sems, self.anyone = send_sems, recv_sems, anyone
        self.count = 0
        self.sent = []

    def new(self):
        self.count += 1
        return self.count - 1

    def copy(self, number, src, dst, device):
        return pltpu.make_async_remote_copy(
            src_ref=src,
            dst_ref=dst,
            send_sem=self.send_sems.at[number],
            recv_sem=self.recv_sems.at[number],
            device_id=device,
            device_id_type=MESH,
        )

    def send(self, number, src, dst, device):
        self.copy(number, src, dst, device).start()
        self.sent.append((number, src, dst, device))

    def recv(self, number, dst):
        self.copy(number, dst, dst, self.anyone).wait_recv()

    def drain(self, numbers=None):
        chosen = [m for m in self.sent if numbers is None or m[0] in numbers]
        self.sent = [m for m in self.sent if m not in chosen]
        for message in chosen:
            self.copy(*message).wait_send()


class Gather:
    def __init__(
        self, wire, at, minus, plus, across, sibling=None, other_at=None, far_z=True
    ):
        self.far_z = far_z
        self.wire, self.at = wire, at
        self.minus, self.plus, self.across = minus, plus, across
        self.sibling, self.other_at = sibling, other_at
        self.ids = {
            name: wire.new()
            for name in ("own_m", "own_p", "own_z", "z_m", "z_p", "fwd_p", "far")
        }
        self.sib_ids = {d: wire.new() for d in ORDER} if sibling is not None else {}

    def push(self, name, d, device):
        ref = self.at(d)
        self.wire.send(self.ids[name], ref, ref, device)

    def share(self, d):
        if self.sibling is not None:
            ref = self.at(d)
            self.wire.send(self.sib_ids[d], ref, ref, self.sibling)

    def take(self, name, d):
        self.wire.recv(self.ids[name], self.at(d))

    def start(self):
        self.push("own_z", (0, 0), self.across)
        self.push("own_m", (0, 0), self.minus)
        self.push("own_p", (0, 0), self.plus)
        self.share((0, 0))

    def z1(self):
        self.take("own_z", (0, 1))
        self.push("z_m", (0, 1), self.minus)
        self.push("z_p", (0, 1), self.plus)
        self.share((0, 1))

    def f1(self):
        self.take("own_p", (-1, 0))
        self.push("fwd_p", (-1, 0), self.plus)
        self.share((-1, 0))

    def g1(self):
        if self.far_z:
            self.take("fwd_p", (2, 0))
            self.push("far", (2, 0), self.across)
            self.share((2, 0))
        else:
            self.take("z_m", (1, 1))
            self.push("far", (1, 1), self.minus)
            self.share((1, 1))

    def rest(self):
        self.take("own_m", (1, 0))
        self.share((1, 0))
        self.take("z_p", (-1, 1))
        self.share((-1, 1))
        if self.far_z:
            self.take("z_m", (1, 1))
            self.share((1, 1))

    def last(self):
        if not self.far_z:
            self.take("fwd_p", (2, 0))
            self.share((2, 0))
        self.take("far", (2, 1))
        self.share((2, 1))

    def sib(self):
        for d in ORDER:
            self.wire.recv(self.sib_ids[d], self.other_at(d))


class Reduce:
    def __init__(self, wire, part, got, minus, plus, across):
        self.wire, self.part, self.got = wire, part, got
        self.minus, self.plus, self.across = minus, plus, across
        self.ids = [wire.new() for _ in range(7)]

    def push(self, index, d, device):
        self.wire.send(self.ids[index], self.part(ORDER.index(d)), self.got.at[index], device)

    def add(self, d, *indices):
        term = self.part(ORDER.index(d))[...].astype(F32)
        for index in indices:
            self.wire.recv(self.ids[index], self.got.at[index])
            term = term + self.got[index].astype(F32)
        return term

    def store(self, d, term):
        self.part(ORDER.index(d))[...] = term.astype(BF)

    def p0(self):
        self.push(0, (2, 1), self.across)

    def p1(self):
        self.push(2, (1, 1), self.plus)
        self.push(3, (-1, 1), self.minus)

    def p2(self):
        self.push(4, (1, 0), self.plus)

    def t20(self):
        self.store((2, 0), self.add((2, 0), 0))
        self.push(1, (2, 0), self.minus)

    def tm10(self):
        self.store((-1, 0), self.add((-1, 0), 1))
        self.push(5, (-1, 0), self.minus)

    def s01(self):
        self.store((0, 1), self.add((0, 1), 2, 3))
        self.push(6, (0, 1), self.across)

    def final(self):
        return self.add((0, 0), 4, 6, 5)


N_MESSAGES = 3 * 15 + 3 * 2 * 7 + 2 * 7 + 2 * (8 + 7) + 4
N_LOCAL = 7


def kernel(
    levels,
    mask_row,
    inputs,
    upstream,
    gate_saved,
    up_saved,
    gate_weight,
    up_weight,
    down_weight,
    out_in,
    out_gate,
    out_up,
    out_down,
    w_all,
    in_all,
    h_all,
    g_all,
    u_all,
    gw,
    uw,
    dw,
    up_own,
    in_own,
    gs,
    us,
    h_part,
    h_got,
    q_part,
    q_sib,
    q_got,
    q_acc,
    acc_down,
    acc_gate,
    acc_up,
    count,
    send_sems,
    recv_sems,
    local_sems,
):
    row, col = lax.axis_index("row"), lax.axis_index("col")
    z_lo, x, core = row // 8, (row // 2) % 4, row % 2
    y, z_hi = col // 2, col % 2
    sign = 1 - 2 * core

    def row_of(z, x_at, k):
        return z * 8 + lax.rem(x_at + 8, 4) * 2 + k

    def col_of(y_at, z):
        return lax.rem(y_at + 8, 4) * 2 + z

    sibling = (row_of(z_lo, x, 1 - core), col)
    row_z = (row_of(1 - z_lo, x, core), col)
    row_m, row_p = (row_of(z_lo, x - sign, core), col), (row_of(z_lo, x + sign, core), col)
    col_z = (row, col_of(y, 1 - z_hi))
    col_m, col_p = (row, col_of(y - sign, z_hi)), (row, col_of(y + sign, z_hi))

    def flip(bit, d):
        return 1 - bit if d else bit

    def chip_at(d, turned=False):
        step = -d[0] if turned else d[0]
        return flip(z_lo, d[1]) * 4 + lax.rem(x + sign * step + 8, 4)

    def row_slot(d, k=core):
        return 2 * chip_at(d) + k

    def col_at(d, turned=False):
        step = -d[0] if turned else d[0]
        return col_of(y + sign * step, flip(z_hi, d[1]))

    def ring(minus, plus, turned):
        return (plus, minus) if turned else (minus, plus)

    loads = {}
    for number, (name, src, dst) in enumerate(
        (
            ("upstream", upstream, up_own),
            ("gs", gate_saved, gs),
            ("us", up_saved, us),
            ("inputs", inputs, in_own),
            ("dw", down_weight, dw),
            ("gw", gate_weight, gw),
            ("uw", up_weight, uw),
        )
    ):
        loads[name] = pltpu.make_async_copy(src, dst, local_sems.at[number])
        loads[name].start()

    barrier = pltpu.get_barrier_semaphore()
    neighbours = (sibling, row_z, row_m, row_p, col_z, col_m, col_p)
    for device in neighbours:
        pl.semaphore_signal(barrier, inc=1, device_id=device, device_id_type=MESH)

    flags = jnp.transpose(jnp.broadcast_to(mask_row[...].astype(F32), (128, 128)))
    noise = jnp.full((1, 128), levels[row * 128 // SEQ], jnp.int32).astype(F32) / 1000.0
    factor = flags / noise
    loads["upstream"].wait()
    w_all[row] = (up_own[...].astype(F32) * jnp.concatenate([factor] * 8, axis=1)).astype(BF)
    count[0] = jnp.broadcast_to(jnp.sum(flags, axis=0, keepdims=True), (8, 128))

    pl.semaphore_wait(barrier, len(neighbours))

    wire = Wire(send_sems, recv_sems, sibling)
    def row_gather(view, far_z):
        return Gather(
            wire,
            lambda d: view(row_slot(d)),
            row_m,
            row_p,
            row_z,
            sibling,
            lambda d: view(row_slot(d, 1 - core)),
            far_z,
        )

    def col_gather(buf, half, far_z, turned):
        def at(d):
            return buf.at[2 * col_at(d, turned) + half]

        return Gather(wire, at, *ring(col_m, col_p, turned), col_z, far_z=far_z)

    W0 = row_gather(lambda slot: w_all.at[slot, pl.ds(0, 64)], False)
    W1 = row_gather(lambda slot: w_all.at[slot, pl.ds(64, 64)], False)
    I = row_gather(lambda slot: in_all.at[slot], False)
    H0 = col_gather(h_all, 0, False, True)
    H1 = col_gather(h_all, 1, False, True)
    G0 = col_gather(g_all, 0, True, False)
    G1 = col_gather(g_all, 1, True, False)
    U0 = col_gather(u_all, 0, True, True)
    U1 = col_gather(u_all, 1, True, False)

    step = 1 - 2 * lax.rem(x, 2)
    partners = (
        sibling,
        row_z,
        (row_of(z_lo, x + step, core), col),
        (row_of(z_lo, x - step, core), col),
    )
    count_ids = [wire.new() for _ in partners]

    def count_send(stage):
        wire.send(count_ids[stage], count.at[2 * stage], count.at[2 * stage + 1], partners[stage])

    def count_recv(stage):
        wire.recv(count_ids[stage], count.at[2 * stage + 1])
        count[2 * stage + 2] = count[2 * stage] + count[2 * stage + 1]

    def saved(parts):
        gate_f = jnp.concatenate([gs[at, :] for at in parts], axis=0).astype(F32)
        up_f = jnp.concatenate([us[at, :] for at in parts], axis=0).astype(F32)
        sigmoid_gate = jax.nn.sigmoid(gate_f)
        return gate_f, up_f, sigmoid_gate, sigmoid_gate * gate_f

    def hidden(half):
        _, up_f, _, silu_gate = saved([pl.ds(half * 128, 128)])
        values = (silu_gate * up_f).astype(BF).astype(F32)
        h_all[2 * col + half] = jnp.transpose(values).astype(BF)

    class ColReduce(Reduce):
        def __init__(self, half, turned):
            self.half, self.turned = half, turned
            super().__init__(
                wire,
                lambda index: h_part.at[half, index],
                h_got.at[half],
                *ring(col_m, col_p, turned),
                col_z,
            )

        def c(self, pair):
            ds = ORDER[2 * pair : 2 * pair + 2]
            at = pl.ds(64 * self.half, 64)
            rows = jnp.concatenate(
                [w_all[2 * col_at(d, self.turned) + k, at, :] for d in ds for k in range(2)], axis=0
            )
            term = lax.dot_general(rows, dw[...], NT, preferred_element_type=F32).astype(BF)
            h_part[self.half, 2 * pair] = term[:128]
            h_part[self.half, 2 * pair + 1] = term[128:]
            if pair < 3:
                (self.p0, self.p1, self.p2)[pair]()

    def hidden_grads(half, reduce, gather):
        scale = 2048.0 / count[8][0:1, 0:1]
        hidden_grad = scale * reduce.final()
        gate_f, up_f, sigmoid_gate, silu_gate = saved(
            [pl.ds(128 * k + 64 * half, 64) for k in range(2)]
        )
        g_all[2 * col + half] = (
            hidden_grad * up_f * sigmoid_gate * (1.0 + gate_f * (1.0 - sigmoid_gate))
        ).astype(BF)
        gather.start()
        u_all[2 * col + half] = (hidden_grad * silu_gate).astype(BF)

    def down(half, tile):
        at = pl.ds(tile * 224, 224)
        lhs = jnp.concatenate([h_all[2 * c + half, at, :] for c in range(8)], axis=1)
        rhs = jnp.concatenate([w_all[2 * c + half] for c in range(8)], axis=0)
        term = jnp.dot(lhs, rhs, preferred_element_type=F32)
        if half == 0:
            acc_down[at, :] = term
        else:
            scale = 2048.0 / count[8][0:1, 0:1]
            out_down[at, :] = (scale * (acc_down[at, :] + term)).astype(BF)

    def regroup():
        wire.drain(list(I.ids.values()) + list(I.sib_ids.values()))
        for c in range(8):
            first, second = in_all[2 * c], in_all[2 * c + 1]
            in_all[2 * c] = jnp.concatenate([first[:, :64], second[:, :64]], axis=1)
            in_all[2 * c + 1] = jnp.concatenate([first[:, 64:], second[:, 64:]], axis=1)

    def weight(half, tile, grads, acc, out):
        at = pl.ds(tile * 256, 256)
        lhs = jnp.concatenate([in_all[2 * c + half, at, :] for c in range(8)], axis=1)
        rhs = jnp.concatenate([grads[2 * c + half] for c in range(8)], axis=0)
        term = jnp.dot(lhs, rhs, preferred_element_type=F32)
        if half == 0:
            acc[at, :] = term
        else:
            out[at, :] = (acc[at, :] + term).astype(BF)

    class RowReduce(Reduce):
        def __init__(self, half, turned):
            self.half, self.turned = half, turned
            self.sib_ids = [wire.new() for _ in ORDER]
            super().__init__(
                wire,
                lambda index: q_part.at[half, index, core],
                q_got.at[half],
                *ring(row_m, row_p, turned),
                row_z,
            )

        def rows(self, grads, pair):
            ds = ORDER[2 * pair : 2 * pair + 2]
            slots = [2 * chip_at(d, self.turned) + self.half for d in ds]
            return jnp.concatenate([grads[slot] for slot in slots], axis=0)

        def a(self, pair):
            q_acc[pair] = lax.dot_general(
                self.rows(g_all, pair), gw[...], NT, preferred_element_type=F32
            )

        def c(self, pair):
            term = q_acc[pair] + lax.dot_general(
                self.rows(u_all, pair), uw[...], NT, preferred_element_type=F32
            )
            for part in range(4):
                q_part[self.half, 2 * pair + part // 2, part % 2] = term[
                    64 * part : 64 * part + 64
                ].astype(BF)
            for index in (2 * pair, 2 * pair + 1):
                there = MIRROR[index]
                wire.send(
                    self.sib_ids[there],
                    q_part.at[self.half, index, 1 - core],
                    q_sib.at[self.half, there],
                    sibling,
                )

        def k(self, pair):
            for index in (2 * pair, 2 * pair + 1):
                wire.recv(self.sib_ids[index], q_sib.at[self.half, index])
                own = self.part(index)
                own[...] = (
                    own[...].astype(F32) + q_sib[self.half, index].astype(F32)
                ).astype(BF)
            if pair < 3:
                (self.p0, self.p1, self.p2)[pair]()

        def fin(self):
            out_in[pl.ds(64 * self.half, 64), :] = self.final().astype(BF)

    R0, R1 = ColReduce(0, False), ColReduce(1, False)
    Q0, Q1 = RowReduce(0, True), RowReduce(1, False)

    W0.start()
    count_send(0)
    loads["inputs"].wait()
    in_all[row] = jnp.transpose(in_own[...].astype(F32)).astype(BF)
    loads["gs"].wait()
    loads["us"].wait()
    hidden(0)
    H0.start()
    W1.start()
    hidden(1)
    W0.z1()
    count_recv(0)
    count_send(1)
    H1.start()
    W0.f1()
    H0.f1()
    W0.g1()
    W1.f1()
    H0.z1()
    W0.rest()
    W1.z1()
    W0.last()
    count_recv(1)
    count_send(2)
    W0.sib()
    loads["dw"].wait()
    R0.c(0)
    H0.g1()
    W1.rest()
    W1.g1()
    I.start()
    R0.c(1)
    count_recv(2)
    count_send(3)
    W1.last()
    H0.rest()
    R0.t20()
    R0.c(2)
    W1.sib()
    R0.c(3)
    H0.last()
    R1.c(0)
    R1.c(1)
    I.z1()
    R1.c(2)
    R0.s01()
    down(0, 1)
    R0.tm10()
    R1.c(3)
    down(0, 3)
    I.f1()
    I.g1()
    R1.t20()
    down(0, 2)
    count_recv(3)
    hidden_grads(0, R0, G0)
    U0.start()
    R1.s01()
    down(0, 0)
    R1.tm10()
    G0.f1()
    I.rest()
    G0.z1()
    I.last()
    I.sib()
    U0.f1()
    regroup()
    G0.g1()
    U0.z1()
    hidden_grads(1, R1, G1)
    G0.rest()
    G0.last()
    weight(0, 3, g_all, acc_gate, out_gate)
    weight(0, 1, g_all, acc_gate, out_gate)
    loads["gw"].wait()
    loads["uw"].wait()
    Q0.a(0)
    U0.g1()
    U1.start()
    Q0.a(1)
    Q0.a(2)
    G1.f1()
    U0.rest()
    weight(0, 2, g_all, acc_gate, out_gate)
    U0.last()
    Q0.c(0)
    U1.f1()
    Q0.c(1)
    Q0.k(0)
    Q0.a(3)
    G1.z1()
    Q0.c(2)
    U1.z1()
    weight(0, 1, u_all, acc_up, out_up)
    G1.g1()
    Q0.c(3)
    H1.z1()
    Q0.k(2)
    H1.f1()
    weight(0, 0, u_all, acc_up, out_up)
    Q0.k(1)
    weight(0, 3, u_all, acc_up, out_up)
    Q0.k(3)
    weight(0, 2, u_all, acc_up, out_up)
    weight(0, 0, g_all, acc_gate, out_gate)
    U1.g1()
    Q0.t20()
    G1.rest()
    G1.last()
    Q1.a(0)
    Q1.a(1)
    Q0.s01()
    Q1.a(2)
    Q1.a(3)
    weight(1, 0, g_all, acc_gate, out_gate)
    U1.rest()
    U1.last()
    Q1.c(0)
    Q1.c(1)
    Q1.c(2)
    Q0.tm10()
    Q1.k(0)
    weight(1, 0, u_all, acc_up, out_up)
    Q1.k(1)
    H1.g1()
    weight(1, 1, g_all, acc_gate, out_gate)
    Q1.c(3)
    weight(1, 1, u_all, acc_up, out_up)
    H1.rest()
    Q1.t20()
    Q1.k(2)
    Q0.fin()
    weight(1, 2, u_all, acc_up, out_up)
    weight(1, 3, u_all, acc_up, out_up)
    Q1.k(3)
    Q1.s01()
    H1.last()
    down(1, 0)
    Q1.tm10()
    weight(1, 2, g_all, acc_gate, out_gate)
    weight(1, 3, g_all, acc_gate, out_gate)
    down(1, 1)
    down(1, 2)
    down(1, 3)
    Q1.fin()
    wire.drain()
    assert wire.count == N_MESSAGES, wire.count


def shards(
    inputs, upstream, mask_flags, levels, gate_saved, up_saved, gate_weight, up_weight, down_weight
):
    anywhere = pl.BlockSpec(memory_space=pl.ANY)
    results = (
        jax.ShapeDtypeStruct((128, 1024), BF),
        jax.ShapeDtypeStruct((1024, 896), BF),
        jax.ShapeDtypeStruct((1024, 896), BF),
        jax.ShapeDtypeStruct((896, 1024), BF),
    )
    inside = pl.BlockSpec(memory_space=pltpu.VMEM)
    return pl.pallas_call(
        kernel,
        out_shape=tuple(pltpu.VMEM(result.shape, BF) for result in results),
        in_specs=[
            pl.BlockSpec(memory_space=pltpu.SMEM),
            pl.BlockSpec(memory_space=pltpu.VMEM),
        ]
        + [anywhere] * 7,
        out_specs=(inside,) * 4,
        scratch_shapes=[
            pltpu.VMEM((16, 128, 1024), BF),
            pltpu.VMEM((16, 1024, 128), BF),
            pltpu.VMEM((16, 896, 128), BF),
            pltpu.VMEM((16, 128, 896), BF),
            pltpu.VMEM((16, 128, 896), BF),
            pltpu.VMEM((1024, 896), BF),
            pltpu.VMEM((1024, 896), BF),
            pltpu.VMEM((896, 1024), BF),
            pltpu.VMEM((128, 1024), BF),
            pltpu.VMEM((128, 1024), BF),
            pltpu.VMEM((256, 896), BF),
            pltpu.VMEM((256, 896), BF),
            pltpu.VMEM((2, 8, 128, 896), BF),
            pltpu.VMEM((2, 7, 128, 896), BF),
            pltpu.VMEM((2, 8, 2, 64, 1024), BF),
            pltpu.VMEM((2, 8, 64, 1024), BF),
            pltpu.VMEM((2, 7, 64, 1024), BF),
            pltpu.VMEM((4, 256, 1024), F32),
            pltpu.VMEM((896, 1024), F32),
            pltpu.VMEM((1024, 896), F32),
            pltpu.VMEM((1024, 896), F32),
            pltpu.VMEM((9, 8, 128), F32),
            pltpu.SemaphoreType.DMA((N_MESSAGES,)),
            pltpu.SemaphoreType.DMA((N_MESSAGES,)),
            pltpu.SemaphoreType.DMA((N_LOCAL,)),
        ],
        compiler_params=pltpu.CompilerParams(
            collective_id=0, has_side_effects=True, vmem_limit_bytes=56 * 2**20
        ),
        cost_estimate=pl.CostEstimate(
            flops=12 * 2048 * 1024 * 896, bytes_accessed=16 * 2**20, transcendentals=2 * 256 * 896
        ),
        name="swiglu_backward",
    )(
        levels,
        mask_flags.reshape(1, -1),
        inputs,
        upstream,
        gate_saved,
        up_saved,
        gate_weight,
        up_weight,
        down_weight,
    )


def solution(mesh):
    placed = (
        P("row", "col"),
        P("row", "col"),
        P("row"),
        P(),
        P("col", "row"),
        P("col", "row"),
        P("col", "row"),
        P("col", "row"),
        P("row", "col"),
    )
    return jax.shard_map(
        shards,
        mesh=mesh,
        in_specs=placed,
        out_specs=(P("row", "col"), P("col", "row"), P("col", "row"), P("row", "col")),
        check_vma=False,
    )
```

```python
import jax
import jax.numpy as jnp
from jax import lax
from jax.experimental import pallas as pl
from jax.experimental.pallas import tpu as pltpu
from jax.sharding import PartitionSpec as P

SEQ = 512
BF = jnp.bfloat16
F32 = jnp.float32
MESH = pl.DeviceIdType.MESH
NT = (((1,), (1,)), ((), ()))
MIRROR = (0, 1, 3, 2, 5, 4, 6, 7)
ORDER = ((2, 1), (2, 0), (1, 1), (-1, 1), (1, 0), (-1, 0), (0, 1), (0, 0))


class Wire:
    def __init__(self, send_sems, recv_sems, anyone):
        self.send_sems, self.recv_sems, self.anyone = send_sems, recv_sems, anyone
        self.count = 0
        self.sent = []

    def new(self):
        self.count += 1
        return self.count - 1

    def copy(self, number, src, dst, device):
        return pltpu.make_async_remote_copy(
            src_ref=src,
            dst_ref=dst,
            send_sem=self.send_sems.at[number],
            recv_sem=self.recv_sems.at[number],
            device_id=device,
            device_id_type=MESH,
        )

    def send(self, number, src, dst, device):
        self.copy(number, src, dst, device).start()
        self.sent.append((number, src, dst, device))

    def recv(self, number, dst):
        self.copy(number, dst, dst, self.anyone).wait_recv()

    def drain(self, numbers=None):
        chosen = [m for m in self.sent if numbers is None or m[0] in numbers]
        self.sent = [m for m in self.sent if m not in chosen]
        for message in chosen:
            self.copy(*message).wait_send()


class Gather:
    def __init__(
        self, wire, at, minus, plus, across, sibling=None, other_at=None, far_z=True
    ):
        self.far_z = far_z
        self.wire, self.at = wire, at
        self.minus, self.plus, self.across = minus, plus, across
        self.sibling, self.other_at = sibling, other_at
        self.ids = {
            name: wire.new()
            for name in ("own_m", "own_p", "own_z", "z_m", "z_p", "fwd_p", "far")
        }
        self.sib_ids = {d: wire.new() for d in ORDER} if sibling is not None else {}

    def push(self, name, d, device):
        ref = self.at(d)
        self.wire.send(self.ids[name], ref, ref, device)

    def share(self, d):
        if self.sibling is not None:
            ref = self.at(d)
            self.wire.send(self.sib_ids[d], ref, ref, self.sibling)

    def take(self, name, d):
        self.wire.recv(self.ids[name], self.at(d))

    def start(self):
        self.push("own_z", (0, 0), self.across)
        self.push("own_m", (0, 0), self.minus)
        self.push("own_p", (0, 0), self.plus)
        self.share((0, 0))

    def z1(self):
        self.take("own_z", (0, 1))
        self.push("z_m", (0, 1), self.minus)
        self.push("z_p", (0, 1), self.plus)
        self.share((0, 1))

    def f1(self):
        self.take("own_p", (-1, 0))
        self.push("fwd_p", (-1, 0), self.plus)
        self.share((-1, 0))

    def g1(self):
        if self.far_z:
            self.take("fwd_p", (2, 0))
            self.push("far", (2, 0), self.across)
            self.share((2, 0))
        else:
            self.take("z_m", (1, 1))
            self.push("far", (1, 1), self.minus)
            self.share((1, 1))

    def rest(self):
        self.take("own_m", (1, 0))
        self.share((1, 0))
        self.take("z_p", (-1, 1))
        self.share((-1, 1))
        if self.far_z:
            self.take("z_m", (1, 1))
            self.share((1, 1))

    def last(self):
        if not self.far_z:
            self.take("fwd_p", (2, 0))
            self.share((2, 0))
        self.take("far", (2, 1))
        self.share((2, 1))

    def sib(self):
        for d in ORDER:
            self.wire.recv(self.sib_ids[d], self.other_at(d))


class Reduce:
    def __init__(self, wire, part, got, minus, plus, across):
        self.wire, self.part, self.got = wire, part, got
        self.minus, self.plus, self.across = minus, plus, across
        self.ids = [wire.new() for _ in range(7)]

    def push(self, index, d, device):
        self.wire.send(self.ids[index], self.part(ORDER.index(d)), self.got.at[index], device)

    def add(self, d, *indices):
        term = self.part(ORDER.index(d))[...].astype(F32)
        for index in indices:
            self.wire.recv(self.ids[index], self.got.at[index])
            term = term + self.got[index].astype(F32)
        return term

    def store(self, d, term):
        self.part(ORDER.index(d))[...] = term.astype(BF)

    def p0(self):
        self.push(0, (2, 1), self.across)

    def p1(self):
        self.push(2, (1, 1), self.plus)
        self.push(3, (-1, 1), self.minus)

    def p2(self):
        self.push(4, (1, 0), self.plus)

    def t20(self):
        self.store((2, 0), self.add((2, 0), 0))
        self.push(1, (2, 0), self.minus)

    def tm10(self):
        self.store((-1, 0), self.add((-1, 0), 1))
        self.push(5, (-1, 0), self.minus)

    def s01(self):
        self.store((0, 1), self.add((0, 1), 2, 3))
        self.push(6, (0, 1), self.across)

    def final(self):
        return self.add((0, 0), 4, 6, 5)


N_MESSAGES = 3 * 15 + 3 * 2 * 7 + 2 * 7 + 2 * (8 + 7) + 4
N_LOCAL = 7


def kernel(
    levels,
    mask_row,
    inputs,
    upstream,
    gate_saved,
    up_saved,
    gate_weight,
    up_weight,
    down_weight,
    out_in,
    out_gate,
    out_up,
    out_down,
    w_all,
    in_all,
    h_all,
    g_all,
    u_all,
    gw,
    uw,
    dw,
    up_own,
    in_own,
    gs,
    us,
    h_part,
    h_got,
    q_part,
    q_sib,
    q_got,
    q_acc,
    acc_down,
    acc_gate,
    acc_up,
    count,
    send_sems,
    recv_sems,
    local_sems,
):
    row, col = lax.axis_index("row"), lax.axis_index("col")
    z_lo, x, core = row // 8, (row // 2) % 4, row % 2
    y, z_hi = col // 2, col % 2
    sign = 1 - 2 * core

    def row_of(z, x_at, k):
        return z * 8 + lax.rem(x_at + 8, 4) * 2 + k

    def col_of(y_at, z):
        return lax.rem(y_at + 8, 4) * 2 + z

    sibling = (row_of(z_lo, x, 1 - core), col)
    row_z = (row_of(1 - z_lo, x, core), col)
    row_m, row_p = (row_of(z_lo, x - sign, core), col), (row_of(z_lo, x + sign, core), col)
    col_z = (row, col_of(y, 1 - z_hi))
    col_m, col_p = (row, col_of(y - sign, z_hi)), (row, col_of(y + sign, z_hi))

    def flip(bit, d):
        return 1 - bit if d else bit

    def chip_at(d, turned=False):
        step = -d[0] if turned else d[0]
        return flip(z_lo, d[1]) * 4 + lax.rem(x + sign * step + 8, 4)

    def row_slot(d, k=core):
        return 2 * chip_at(d) + k

    def col_at(d, turned=False):
        step = -d[0] if turned else d[0]
        return col_of(y + sign * step, flip(z_hi, d[1]))

    def ring(minus, plus, turned):
        return (plus, minus) if turned else (minus, plus)

    loads = {}
    for number, (name, src, dst) in enumerate(
        (
            ("upstream", upstream, up_own),
            ("gs", gate_saved, gs),
            ("us", up_saved, us),
            ("inputs", inputs, in_own),
            ("dw", down_weight, dw),
            ("gw", gate_weight, gw),
            ("uw", up_weight, uw),
        )
    ):
        loads[name] = pltpu.make_async_copy(src, dst, local_sems.at[number])
        loads[name].start()

    barrier = pltpu.get_barrier_semaphore()
    neighbours = (sibling, row_z, row_m, row_p, col_z, col_m, col_p)
    for device in neighbours:
        pl.semaphore_signal(barrier, inc=1, device_id=device, device_id_type=MESH)

    flags = jnp.transpose(jnp.broadcast_to(mask_row[...].astype(F32), (128, 128)))
    noise = jnp.full((1, 128), levels[row * 128 // SEQ], jnp.int32).astype(F32) / 1000.0
    factor = flags / noise
    loads["upstream"].wait()
    w_all[row] = (up_own[...].astype(F32) * jnp.concatenate([factor] * 8, axis=1)).astype(BF)
    count[0] = jnp.broadcast_to(jnp.sum(flags, axis=0, keepdims=True), (8, 128))

    pl.semaphore_wait(barrier, len(neighbours))

    wire = Wire(send_sems, recv_sems, sibling)
    def row_gather(view, far_z):
        return Gather(
            wire,
            lambda d: view(row_slot(d)),
            row_m,
            row_p,
            row_z,
            sibling,
            lambda d: view(row_slot(d, 1 - core)),
            far_z,
        )

    def col_gather(buf, half, far_z, turned):
        def at(d):
            return buf.at[2 * col_at(d, turned) + half]

        return Gather(wire, at, *ring(col_m, col_p, turned), col_z, far_z=far_z)

    W0 = row_gather(lambda slot: w_all.at[slot, pl.ds(0, 64)], False)
    W1 = row_gather(lambda slot: w_all.at[slot, pl.ds(64, 64)], False)
    I = row_gather(lambda slot: in_all.at[slot], False)
    H0 = col_gather(h_all, 0, False, True)
    H1 = col_gather(h_all, 1, False, True)
    G0 = col_gather(g_all, 0, True, False)
    G1 = col_gather(g_all, 1, True, False)
    U0 = col_gather(u_all, 0, True, True)
    U1 = col_gather(u_all, 1, True, False)

    step = 1 - 2 * lax.rem(x, 2)
    partners = (
        sibling,
        row_z,
        (row_of(z_lo, x + step, core), col),
        (row_of(z_lo, x - step, core), col),
    )
    count_ids = [wire.new() for _ in partners]

    def count_send(stage):
        wire.send(count_ids[stage], count.at[2 * stage], count.at[2 * stage + 1], partners[stage])

    def count_recv(stage):
        wire.recv(count_ids[stage], count.at[2 * stage + 1])
        count[2 * stage + 2] = count[2 * stage] + count[2 * stage + 1]

    def saved(parts):
        gate_f = jnp.concatenate([gs[at, :] for at in parts], axis=0).astype(F32)
        up_f = jnp.concatenate([us[at, :] for at in parts], axis=0).astype(F32)
        sigmoid_gate = jax.nn.sigmoid(gate_f)
        return gate_f, up_f, sigmoid_gate, sigmoid_gate * gate_f

    def hidden(half):
        _, up_f, _, silu_gate = saved([pl.ds(half * 128, 128)])
        values = (silu_gate * up_f).astype(BF).astype(F32)
        h_all[2 * col + half] = jnp.transpose(values).astype(BF)

    class ColReduce(Reduce):
        def __init__(self, half, turned):
            self.half, self.turned = half, turned
            super().__init__(
                wire,
                lambda index: h_part.at[half, index],
                h_got.at[half],
                *ring(col_m, col_p, turned),
                col_z,
            )

        def c(self, pair):
            ds = ORDER[2 * pair : 2 * pair + 2]
            at = pl.ds(64 * self.half, 64)
            rows = jnp.concatenate(
                [w_all[2 * col_at(d, self.turned) + k, at, :] for d in ds for k in range(2)], axis=0
            )
            term = lax.dot_general(rows, dw[...], NT, preferred_element_type=F32).astype(BF)
            h_part[self.half, 2 * pair] = term[:128]
            h_part[self.half, 2 * pair + 1] = term[128:]
            if pair < 3:
                (self.p0, self.p1, self.p2)[pair]()

    def hidden_grads(half, reduce, gather):
        scale = 2048.0 / count[8][0:1, 0:1]
        hidden_grad = scale * reduce.final()
        gate_f, up_f, sigmoid_gate, silu_gate = saved(
            [pl.ds(128 * k + 64 * half, 64) for k in range(2)]
        )
        g_all[2 * col + half] = (
            hidden_grad * up_f * sigmoid_gate * (1.0 + gate_f * (1.0 - sigmoid_gate))
        ).astype(BF)
        gather.start()
        u_all[2 * col + half] = (hidden_grad * silu_gate).astype(BF)

    def down(half, tile):
        at = pl.ds(tile * 224, 224)
        lhs = jnp.concatenate([h_all[2 * c + half, at, :] for c in range(8)], axis=1)
        rhs = jnp.concatenate([w_all[2 * c + half] for c in range(8)], axis=0)
        term = jnp.dot(lhs, rhs, preferred_element_type=F32)
        if half == 0:
            acc_down[at, :] = term
        else:
            scale = 2048.0 / count[8][0:1, 0:1]
            out_down[at, :] = (scale * (acc_down[at, :] + term)).astype(BF)

    def regroup():
        wire.drain(list(I.ids.values()) + list(I.sib_ids.values()))
        for c in range(8):
            first, second = in_all[2 * c], in_all[2 * c + 1]
            in_all[2 * c] = jnp.concatenate([first[:, :64], second[:, :64]], axis=1)
            in_all[2 * c + 1] = jnp.concatenate([first[:, 64:], second[:, 64:]], axis=1)

    def weight(half, tile, grads, acc, out):
        at = pl.ds(tile * 256, 256)
        lhs = jnp.concatenate([in_all[2 * c + half, at, :] for c in range(8)], axis=1)
        rhs = jnp.concatenate([grads[2 * c + half] for c in range(8)], axis=0)
        term = jnp.dot(lhs, rhs, preferred_element_type=F32)
        if half == 0:
            acc[at, :] = term
        else:
            out[at, :] = (acc[at, :] + term).astype(BF)

    class RowReduce(Reduce):
        def __init__(self, half, turned):
            self.half, self.turned = half, turned
            self.sib_ids = [wire.new() for _ in ORDER]
            super().__init__(
                wire,
                lambda index: q_part.at[half, index, core],
                q_got.at[half],
                *ring(row_m, row_p, turned),
                row_z,
            )

        def rows(self, grads, pair):
            ds = ORDER[2 * pair : 2 * pair + 2]
            slots = [2 * chip_at(d, self.turned) + self.half for d in ds]
            return jnp.concatenate([grads[slot] for slot in slots], axis=0)

        def a(self, pair):
            q_acc[pair] = lax.dot_general(
                self.rows(g_all, pair), gw[...], NT, preferred_element_type=F32
            )

        def c(self, pair):
            term = q_acc[pair] + lax.dot_general(
                self.rows(u_all, pair), uw[...], NT, preferred_element_type=F32
            )
            for part in range(4):
                q_part[self.half, 2 * pair + part // 2, part % 2] = term[
                    64 * part : 64 * part + 64
                ].astype(BF)
            for index in (2 * pair, 2 * pair + 1):
                there = MIRROR[index]
                wire.send(
                    self.sib_ids[there],
                    q_part.at[self.half, index, 1 - core],
                    q_sib.at[self.half, there],
                    sibling,
                )

        def k(self, pair):
            for index in (2 * pair, 2 * pair + 1):
                wire.recv(self.sib_ids[index], q_sib.at[self.half, index])
                own = self.part(index)
                own[...] = (
                    own[...].astype(F32) + q_sib[self.half, index].astype(F32)
                ).astype(BF)
            if pair < 3:
                (self.p0, self.p1, self.p2)[pair]()

        def fin(self):
            out_in[pl.ds(64 * self.half, 64), :] = self.final().astype(BF)

    R0, R1 = ColReduce(0, False), ColReduce(1, False)
    Q0, Q1 = RowReduce(0, True), RowReduce(1, False)

    W0.start()
    count_send(0)
    loads["inputs"].wait()
    in_all[row] = jnp.transpose(in_own[...].astype(F32)).astype(BF)
    loads["gs"].wait()
    loads["us"].wait()
    hidden(0)
    H0.start()
    W1.start()
    hidden(1)
    W0.z1()
    count_recv(0)
    count_send(1)
    H1.start()
    W0.f1()
    H0.f1()
    W0.g1()
    W1.f1()
    H0.z1()
    W0.rest()
    W1.z1()
    W0.last()
    count_recv(1)
    count_send(2)
    W0.sib()
    loads["dw"].wait()
    R0.c(0)
    H0.g1()
    W1.rest()
    W1.g1()
    I.start()
    R0.c(1)
    count_recv(2)
    count_send(3)
    W1.last()
    H0.rest()
    R0.t20()
    R0.c(2)
    W1.sib()
    R0.c(3)
    H0.last()
    R1.c(0)
    R1.c(1)
    I.z1()
    R1.c(2)
    R0.s01()
    down(0, 1)
    R0.tm10()
    R1.c(3)
    down(0, 3)
    I.f1()
    I.g1()
    R1.t20()
    down(0, 2)
    count_recv(3)
    hidden_grads(0, R0, G0)
    U0.start()
    R1.s01()
    down(0, 0)
    R1.tm10()
    G0.f1()
    I.rest()
    G0.z1()
    I.last()
    I.sib()
    U0.f1()
    regroup()
    G0.g1()
    U0.z1()
    hidden_grads(1, R1, G1)
    G0.rest()
    G0.last()
    weight(0, 3, g_all, acc_gate, out_gate)
    weight(0, 1, g_all, acc_gate, out_gate)
    loads["gw"].wait()
    loads["uw"].wait()
    Q0.a(0)
    U0.g1()
    U1.start()
    Q0.a(1)
    Q0.a(2)
    G1.f1()
    U0.rest()
    weight(0, 2, g_all, acc_gate, out_gate)
    U0.last()
    Q0.c(0)
    U1.f1()
    Q0.c(1)
    Q0.k(0)
    Q0.a(3)
    G1.z1()
    Q0.c(2)
    U1.z1()
    weight(0, 1, u_all, acc_up, out_up)
    G1.g1()
    Q0.c(3)
    H1.z1()
    Q0.k(2)
    H1.f1()
    weight(0, 0, u_all, acc_up, out_up)
    Q0.k(1)
    weight(0, 3, u_all, acc_up, out_up)
    Q0.k(3)
    weight(0, 2, u_all, acc_up, out_up)
    weight(0, 0, g_all, acc_gate, out_gate)
    U1.g1()
    Q0.t20()
    G1.rest()
    G1.last()
    Q1.a(0)
    Q1.a(1)
    Q0.s01()
    Q1.a(2)
    Q1.a(3)
    weight(1, 0, g_all, acc_gate, out_gate)
    U1.rest()
    U1.last()
    Q1.c(0)
    Q1.c(1)
    Q1.c(2)
    Q0.tm10()
    Q1.k(0)
    weight(1, 0, u_all, acc_up, out_up)
    Q1.k(1)
    H1.g1()
    weight(1, 1, g_all, acc_gate, out_gate)
    Q1.c(3)
    weight(1, 1, u_all, acc_up, out_up)
    H1.rest()
    Q1.t20()
    Q1.k(2)
    Q0.fin()
    weight(1, 2, u_all, acc_up, out_up)
    weight(1, 3, u_all, acc_up, out_up)
    Q1.k(3)
    Q1.s01()
    H1.last()
    down(1, 0)
    Q1.tm10()
    weight(1, 2, g_all, acc_gate, out_gate)
    weight(1, 3, g_all, acc_gate, out_gate)
    down(1, 1)
    down(1, 2)
    down(1, 3)
    Q1.fin()
    wire.drain()
    assert wire.count == N_MESSAGES, wire.count


def move(*refs):
    sources, results, sems = refs[:4], refs[4:8], refs[8]
    saves = []
    for array in range(4):
        rows = sources[array].shape[0] // 2
        for part in range(2):
            at = pl.ds(part * rows, rows)
            saves.append(
                pltpu.make_async_copy(
                    sources[array].at[at], results[array].at[at], sems.at[2 * array + part]
                )
            )
    for save in saves:
        save.start()
    for save in saves:
        save.wait()


def shards(
    inputs, upstream, mask_flags, levels, gate_saved, up_saved, gate_weight, up_weight, down_weight
):
    anywhere = pl.BlockSpec(memory_space=pl.ANY)
    results = (
        jax.ShapeDtypeStruct((128, 1024), BF),
        jax.ShapeDtypeStruct((1024, 896), BF),
        jax.ShapeDtypeStruct((1024, 896), BF),
        jax.ShapeDtypeStruct((896, 1024), BF),
    )
    inside = pl.BlockSpec(memory_space=pltpu.VMEM)
    grads = pl.pallas_call(
        kernel,
        out_shape=tuple(pltpu.VMEM(result.shape, BF) for result in results),
        in_specs=[
            pl.BlockSpec(memory_space=pltpu.SMEM),
            pl.BlockSpec(memory_space=pltpu.VMEM),
        ]
        + [anywhere] * 7,
        out_specs=(inside,) * 4,
        scratch_shapes=[
            pltpu.VMEM((16, 128, 1024), BF),
            pltpu.VMEM((16, 1024, 128), BF),
            pltpu.VMEM((16, 896, 128), BF),
            pltpu.VMEM((16, 128, 896), BF),
            pltpu.VMEM((16, 128, 896), BF),
            pltpu.VMEM((1024, 896), BF),
            pltpu.VMEM((1024, 896), BF),
            pltpu.VMEM((896, 1024), BF),
            pltpu.VMEM((128, 1024), BF),
            pltpu.VMEM((128, 1024), BF),
            pltpu.VMEM((256, 896), BF),
            pltpu.VMEM((256, 896), BF),
            pltpu.VMEM((2, 8, 128, 896), BF),
            pltpu.VMEM((2, 7, 128, 896), BF),
            pltpu.VMEM((2, 8, 2, 64, 1024), BF),
            pltpu.VMEM((2, 8, 64, 1024), BF),
            pltpu.VMEM((2, 7, 64, 1024), BF),
            pltpu.VMEM((4, 256, 1024), F32),
            pltpu.VMEM((896, 1024), F32),
            pltpu.VMEM((1024, 896), F32),
            pltpu.VMEM((1024, 896), F32),
            pltpu.VMEM((9, 8, 128), F32),
            pltpu.SemaphoreType.DMA((N_MESSAGES,)),
            pltpu.SemaphoreType.DMA((N_MESSAGES,)),
            pltpu.SemaphoreType.DMA((N_LOCAL,)),
        ],
        compiler_params=pltpu.CompilerParams(
            collective_id=0, has_side_effects=True, vmem_limit_bytes=56 * 2**20
        ),
        cost_estimate=pl.CostEstimate(
            flops=12 * 2048 * 1024 * 896, bytes_accessed=16 * 2**20, transcendentals=2 * 256 * 896
        ),
        name="swiglu_backward",
    )(
        levels,
        mask_flags.reshape(1, -1),
        inputs,
        upstream,
        gate_saved,
        up_saved,
        gate_weight,
        up_weight,
        down_weight,
    )
    return pl.pallas_call(
        move,
        out_shape=results,
        in_specs=[inside] * 4,
        out_specs=(anywhere,) * 4,
        scratch_shapes=[pltpu.SemaphoreType.DMA((8,))],
        compiler_params=pltpu.CompilerParams(vmem_limit_bytes=56 * 2**20),
        name="move_results",
    )(*[pltpu.with_memory_space_constraint(grad, pltpu.VMEM) for grad in grads])


def solution(mesh):
    placed = (
        P("row", "col"),
        P("row", "col"),
        P("row"),
        P(),
        P("col", "row"),
        P("col", "row"),
        P("col", "row"),
        P("col", "row"),
        P("row", "col"),
    )
    return jax.shard_map(
        shards,
        mesh=mesh,
        in_specs=placed,
        out_specs=(P("row", "col"), P("col", "row"), P("col", "row"), P("row", "col")),
        check_vma=False,
    )
```

```python
import jax
import jax.numpy as jnp
from jax import lax
from jax.experimental import pallas as pl
from jax.experimental.pallas import tpu as pltpu
from jax.sharding import PartitionSpec as P

SEQ = 512
BF = jnp.bfloat16
F32 = jnp.float32
MESH = pl.DeviceIdType.MESH
NT = (((1,), (1,)), ((), ()))
MIRROR = (0, 1, 3, 2, 5, 4, 6, 7)
ORDER = ((2, 1), (2, 0), (1, 1), (-1, 1), (1, 0), (-1, 0), (0, 1), (0, 0))


class Wire:
    def __init__(self, send_sems, recv_sems, anyone):
        self.send_sems, self.recv_sems, self.anyone = send_sems, recv_sems, anyone
        self.count = 0
        self.sent = []

    def new(self):
        self.count += 1
        return self.count - 1

    def copy(self, number, src, dst, device):
        return pltpu.make_async_remote_copy(
            src_ref=src,
            dst_ref=dst,
            send_sem=self.send_sems.at[number],
            recv_sem=self.recv_sems.at[number],
            device_id=device,
            device_id_type=MESH,
        )

    def send(self, number, src, dst, device):
        self.copy(number, src, dst, device).start()
        self.sent.append((number, src, dst, device))

    def recv(self, number, dst):
        self.copy(number, dst, dst, self.anyone).wait_recv()

    def drain(self, numbers=None):
        chosen = [m for m in self.sent if numbers is None or m[0] in numbers]
        self.sent = [m for m in self.sent if m not in chosen]
        for message in chosen:
            self.copy(*message).wait_send()


class Gather:
    def __init__(
        self, wire, at, minus, plus, across, sibling=None, other_at=None, far_z=True
    ):
        self.far_z = far_z
        self.wire, self.at = wire, at
        self.minus, self.plus, self.across = minus, plus, across
        self.sibling, self.other_at = sibling, other_at
        self.ids = {
            name: wire.new()
            for name in ("own_m", "own_p", "own_z", "z_m", "z_p", "fwd_p", "far")
        }
        self.sib_ids = {d: wire.new() for d in ORDER} if sibling is not None else {}

    def push(self, name, d, device):
        ref = self.at(d)
        self.wire.send(self.ids[name], ref, ref, device)

    def share(self, d):
        if self.sibling is not None:
            ref = self.at(d)
            self.wire.send(self.sib_ids[d], ref, ref, self.sibling)

    def take(self, name, d):
        self.wire.recv(self.ids[name], self.at(d))

    def start(self):
        self.push("own_z", (0, 0), self.across)
        self.push("own_m", (0, 0), self.minus)
        self.push("own_p", (0, 0), self.plus)
        self.share((0, 0))

    def z1(self):
        self.take("own_z", (0, 1))
        self.push("z_m", (0, 1), self.minus)
        self.push("z_p", (0, 1), self.plus)
        self.share((0, 1))

    def f1(self):
        self.take("own_p", (-1, 0))
        self.push("fwd_p", (-1, 0), self.plus)
        self.share((-1, 0))

    def g1(self):
        if self.far_z:
            self.take("fwd_p", (2, 0))
            self.push("far", (2, 0), self.across)
            self.share((2, 0))
        else:
            self.take("z_m", (1, 1))
            self.push("far", (1, 1), self.minus)
            self.share((1, 1))

    def rest(self):
        self.take("own_m", (1, 0))
        self.share((1, 0))
        self.take("z_p", (-1, 1))
        self.share((-1, 1))
        if self.far_z:
            self.take("z_m", (1, 1))
            self.share((1, 1))

    def last(self):
        if not self.far_z:
            self.take("fwd_p", (2, 0))
            self.share((2, 0))
        self.take("far", (2, 1))
        self.share((2, 1))

    def sib(self):
        for d in ORDER:
            self.wire.recv(self.sib_ids[d], self.other_at(d))


class Reduce:
    def __init__(self, wire, part, got, minus, plus, across):
        self.wire, self.part, self.got = wire, part, got
        self.minus, self.plus, self.across = minus, plus, across
        self.ids = [wire.new() for _ in range(7)]

    def push(self, index, d, device):
        self.wire.send(self.ids[index], self.part(ORDER.index(d)), self.got.at[index], device)

    def add(self, d, *indices):
        term = self.part(ORDER.index(d))[...].astype(F32)
        for index in indices:
            self.wire.recv(self.ids[index], self.got.at[index])
            term = term + self.got[index].astype(F32)
        return term

    def store(self, d, term):
        self.part(ORDER.index(d))[...] = term.astype(BF)

    def p0(self):
        self.push(0, (2, 1), self.across)

    def p1(self):
        self.push(2, (1, 1), self.plus)
        self.push(3, (-1, 1), self.minus)

    def p2(self):
        self.push(4, (1, 0), self.plus)

    def t20(self):
        self.store((2, 0), self.add((2, 0), 0))
        self.push(1, (2, 0), self.minus)

    def tm10(self):
        self.store((-1, 0), self.add((-1, 0), 1))
        self.push(5, (-1, 0), self.minus)

    def s01(self):
        self.store((0, 1), self.add((0, 1), 2, 3))
        self.push(6, (0, 1), self.across)

    def final(self):
        return self.add((0, 0), 4, 6, 5)


N_MESSAGES = 3 * 15 + 3 * 2 * 7 + 2 * 7 + 2 * (8 + 7) + 4
N_LOCAL = 7


def kernel(
    levels,
    mask_row,
    inputs,
    upstream,
    gate_saved,
    up_saved,
    gate_weight,
    up_weight,
    down_weight,
    out_in,
    out_gate,
    out_up,
    out_down,
    w_all,
    in_all,
    h_all,
    g_all,
    u_all,
    gw,
    uw,
    dw,
    up_own,
    in_own,
    gs,
    us,
    h_part,
    h_got,
    q_part,
    q_sib,
    q_got,
    q_acc,
    acc_down,
    acc_gate,
    acc_up,
    count,
    send_sems,
    recv_sems,
    local_sems,
):
    row, col = lax.axis_index("row"), lax.axis_index("col")
    z_lo, x, core = row // 8, (row // 2) % 4, row % 2
    y, z_hi = col // 2, col % 2
    sign = 1 - 2 * core

    def row_of(z, x_at, k):
        return z * 8 + lax.rem(x_at + 8, 4) * 2 + k

    def col_of(y_at, z):
        return lax.rem(y_at + 8, 4) * 2 + z

    sibling = (row_of(z_lo, x, 1 - core), col)
    row_z = (row_of(1 - z_lo, x, core), col)
    row_m, row_p = (row_of(z_lo, x - sign, core), col), (row_of(z_lo, x + sign, core), col)
    col_z = (row, col_of(y, 1 - z_hi))
    col_m, col_p = (row, col_of(y - sign, z_hi)), (row, col_of(y + sign, z_hi))

    def flip(bit, d):
        return 1 - bit if d else bit

    def chip_at(d, turned=False):
        step = -d[0] if turned else d[0]
        return flip(z_lo, d[1]) * 4 + lax.rem(x + sign * step + 8, 4)

    def row_slot(d, k=core):
        return 2 * chip_at(d) + k

    def col_at(d, turned=False):
        step = -d[0] if turned else d[0]
        return col_of(y + sign * step, flip(z_hi, d[1]))

    def ring(minus, plus, turned):
        return (plus, minus) if turned else (minus, plus)

    loads = {}
    for number, (name, src, dst) in enumerate(
        (
            ("upstream", upstream, up_own),
            ("gs", gate_saved, gs),
            ("us", up_saved, us),
            ("inputs", inputs, in_own),
            ("dw", down_weight, dw),
            ("gw", gate_weight, gw),
            ("uw", up_weight, uw),
        )
    ):
        loads[name] = pltpu.make_async_copy(src, dst, local_sems.at[number])
        loads[name].start()

    barrier = pltpu.get_barrier_semaphore()
    neighbours = (sibling, row_z, row_m, row_p, col_z, col_m, col_p)
    for device in neighbours:
        pl.semaphore_signal(barrier, inc=1, device_id=device, device_id_type=MESH)

    flags = jnp.transpose(jnp.broadcast_to(mask_row[...].astype(F32), (128, 128)))
    noise = jnp.full((1, 128), levels[row * 128 // SEQ], jnp.int32).astype(F32) / 1000.0
    factor = flags / noise
    loads["upstream"].wait()

    def weigh(at):
        spread = jnp.concatenate([factor[at : at + 64]] * 8, axis=1)
        w_all[row, pl.ds(at, 64), :] = (
            up_own[pl.ds(at, 64), :].astype(F32) * spread
        ).astype(BF)

    weigh(0)
    count[0] = jnp.broadcast_to(jnp.sum(flags, axis=0, keepdims=True), (8, 128))

    pl.semaphore_wait(barrier, len(neighbours))

    wire = Wire(send_sems, recv_sems, sibling)
    def row_gather(view, far_z):
        return Gather(
            wire,
            lambda d: view(row_slot(d)),
            row_m,
            row_p,
            row_z,
            sibling,
            lambda d: view(row_slot(d, 1 - core)),
            far_z,
        )

    def col_gather(buf, half, far_z, turned):
        def at(d):
            return buf.at[2 * col_at(d, turned) + half]

        return Gather(wire, at, *ring(col_m, col_p, turned), col_z, far_z=far_z)

    W0 = row_gather(lambda slot: w_all.at[slot, pl.ds(0, 64)], False)
    W1 = row_gather(lambda slot: w_all.at[slot, pl.ds(64, 64)], False)
    I = row_gather(lambda slot: in_all.at[slot], False)
    H0 = col_gather(h_all, 0, False, True)
    H1 = col_gather(h_all, 1, False, True)
    G0 = col_gather(g_all, 0, True, False)
    G1 = col_gather(g_all, 1, True, False)
    U0 = col_gather(u_all, 0, True, True)
    U1 = col_gather(u_all, 1, True, False)

    step = 1 - 2 * lax.rem(x, 2)
    partners = (
        sibling,
        row_z,
        (row_of(z_lo, x + step, core), col),
        (row_of(z_lo, x - step, core), col),
    )
    count_ids = [wire.new() for _ in partners]

    def count_send(stage):
        wire.send(count_ids[stage], count.at[2 * stage], count.at[2 * stage + 1], partners[stage])

    def count_recv(stage):
        wire.recv(count_ids[stage], count.at[2 * stage + 1])
        count[2 * stage + 2] = count[2 * stage] + count[2 * stage + 1]

    def saved(parts):
        gate_f = jnp.concatenate([gs[at, :] for at in parts], axis=0).astype(F32)
        up_f = jnp.concatenate([us[at, :] for at in parts], axis=0).astype(F32)
        sigmoid_gate = jax.nn.sigmoid(gate_f)
        return gate_f, up_f, sigmoid_gate, sigmoid_gate * gate_f

    def hidden(half):
        _, up_f, _, silu_gate = saved([pl.ds(half * 128, 128)])
        values = (silu_gate * up_f).astype(BF).astype(F32)
        h_all[2 * col + half] = jnp.transpose(values).astype(BF)

    class ColReduce(Reduce):
        def __init__(self, half, turned):
            self.half, self.turned = half, turned
            super().__init__(
                wire,
                lambda index: h_part.at[half, index],
                h_got.at[half],
                *ring(col_m, col_p, turned),
                col_z,
            )

        def c(self, pair):
            ds = ORDER[2 * pair : 2 * pair + 2]
            at = pl.ds(64 * self.half, 64)
            rows = jnp.concatenate(
                [w_all[2 * col_at(d, self.turned) + k, at, :] for d in ds for k in range(2)], axis=0
            )
            term = lax.dot_general(rows, dw[...], NT, preferred_element_type=F32).astype(BF)
            h_part[self.half, 2 * pair] = term[:128]
            h_part[self.half, 2 * pair + 1] = term[128:]
            if pair < 3:
                (self.p0, self.p1, self.p2)[pair]()

    def hidden_grads(half, reduce, gather):
        scale = 2048.0 / count[8][0:1, 0:1]
        hidden_grad = scale * reduce.final()
        gate_f, up_f, sigmoid_gate, silu_gate = saved(
            [pl.ds(128 * k + 64 * half, 64) for k in range(2)]
        )
        g_all[2 * col + half] = (
            hidden_grad * up_f * sigmoid_gate * (1.0 + gate_f * (1.0 - sigmoid_gate))
        ).astype(BF)
        gather.start()
        u_all[2 * col + half] = (hidden_grad * silu_gate).astype(BF)

    def down(half, tile):
        at = pl.ds(tile * 224, 224)
        lhs = jnp.concatenate([h_all[2 * c + half, at, :] for c in range(8)], axis=1)
        rhs = jnp.concatenate([w_all[2 * c + half] for c in range(8)], axis=0)
        term = jnp.dot(lhs, rhs, preferred_element_type=F32)
        if half == 0:
            acc_down[at, :] = term
        else:
            scale = 2048.0 / count[8][0:1, 0:1]
            out_down[at, :] = (scale * (acc_down[at, :] + term)).astype(BF)

    def regroup():
        wire.drain(list(I.ids.values()) + list(I.sib_ids.values()))
        for c in range(8):
            first, second = in_all[2 * c], in_all[2 * c + 1]
            in_all[2 * c] = jnp.concatenate([first[:, :64], second[:, :64]], axis=1)
            in_all[2 * c + 1] = jnp.concatenate([first[:, 64:], second[:, 64:]], axis=1)

    def weight(half, tile, grads, acc, out):
        at = pl.ds(tile * 256, 256)
        lhs = jnp.concatenate([in_all[2 * c + half, at, :] for c in range(8)], axis=1)
        rhs = jnp.concatenate([grads[2 * c + half] for c in range(8)], axis=0)
        term = jnp.dot(lhs, rhs, preferred_element_type=F32)
        if half == 0:
            acc[at, :] = term
        else:
            out[at, :] = (acc[at, :] + term).astype(BF)

    class RowReduce(Reduce):
        def __init__(self, half, turned):
            self.half, self.turned = half, turned
            self.sib_ids = [wire.new() for _ in ORDER]
            super().__init__(
                wire,
                lambda index: q_part.at[half, index, core],
                q_got.at[half],
                *ring(row_m, row_p, turned),
                row_z,
            )

        def rows(self, grads, pair):
            ds = ORDER[2 * pair : 2 * pair + 2]
            slots = [2 * chip_at(d, self.turned) + self.half for d in ds]
            return jnp.concatenate([grads[slot] for slot in slots], axis=0)

        def a(self, pair):
            q_acc[pair] = lax.dot_general(
                self.rows(g_all, pair), gw[...], NT, preferred_element_type=F32
            )

        def c(self, pair):
            term = q_acc[pair] + lax.dot_general(
                self.rows(u_all, pair), uw[...], NT, preferred_element_type=F32
            )
            for part in range(4):
                q_part[self.half, 2 * pair + part // 2, part % 2] = term[
                    64 * part : 64 * part + 64
                ].astype(BF)
            for index in (2 * pair, 2 * pair + 1):
                there = MIRROR[index]
                wire.send(
                    self.sib_ids[there],
                    q_part.at[self.half, index, 1 - core],
                    q_sib.at[self.half, there],
                    sibling,
                )

        def k(self, pair):
            for index in (2 * pair, 2 * pair + 1):
                wire.recv(self.sib_ids[index], q_sib.at[self.half, index])
                own = self.part(index)
                own[...] = (
                    own[...].astype(F32) + q_sib[self.half, index].astype(F32)
                ).astype(BF)
            if pair < 3:
                (self.p0, self.p1, self.p2)[pair]()

        def fin(self):
            out_in[pl.ds(64 * self.half, 64), :] = self.final().astype(BF)

    R0, R1 = ColReduce(0, False), ColReduce(1, False)
    Q0, Q1 = RowReduce(0, True), RowReduce(1, False)

    W0.start()
    weigh(64)
    count_send(0)
    loads["inputs"].wait()
    in_all[row] = jnp.transpose(in_own[...].astype(F32)).astype(BF)
    loads["gs"].wait()
    loads["us"].wait()
    hidden(0)
    H0.start()
    W1.start()
    hidden(1)
    W0.z1()
    count_recv(0)
    count_send(1)
    H1.start()
    W0.f1()
    H0.f1()
    W0.g1()
    W1.f1()
    H0.z1()
    W0.rest()
    W1.z1()
    W0.last()
    count_recv(1)
    count_send(2)
    W0.sib()
    loads["dw"].wait()
    R0.c(0)
    H0.g1()
    W1.rest()
    W1.g1()
    I.start()
    R0.c(1)
    count_recv(2)
    count_send(3)
    W1.last()
    H0.rest()
    R0.t20()
    R0.c(2)
    W1.sib()
    R0.c(3)
    H0.last()
    R1.c(0)
    R1.c(1)
    I.z1()
    R1.c(2)
    R0.s01()
    down(0, 1)
    R0.tm10()
    R1.c(3)
    down(0, 3)
    I.f1()
    I.g1()
    R1.t20()
    down(0, 2)
    count_recv(3)
    hidden_grads(0, R0, G0)
    U0.start()
    R1.s01()
    down(0, 0)
    R1.tm10()
    G0.f1()
    I.rest()
    G0.z1()
    I.last()
    I.sib()
    U0.f1()
    regroup()
    G0.g1()
    U0.z1()
    hidden_grads(1, R1, G1)
    G0.rest()
    G0.last()
    weight(0, 3, g_all, acc_gate, out_gate)
    weight(0, 1, g_all, acc_gate, out_gate)
    loads["gw"].wait()
    loads["uw"].wait()
    Q0.a(0)
    U0.g1()
    U1.start()
    Q0.a(1)
    Q0.a(2)
    G1.f1()
    U0.rest()
    weight(0, 2, g_all, acc_gate, out_gate)
    U0.last()
    Q0.c(0)
    U1.f1()
    Q0.c(1)
    Q0.k(0)
    Q0.a(3)
    G1.z1()
    Q0.c(2)
    U1.z1()
    weight(0, 1, u_all, acc_up, out_up)
    G1.g1()
    Q0.c(3)
    H1.z1()
    Q0.k(2)
    H1.f1()
    weight(0, 0, u_all, acc_up, out_up)
    Q0.k(1)
    weight(0, 3, u_all, acc_up, out_up)
    Q0.k(3)
    weight(0, 2, u_all, acc_up, out_up)
    weight(0, 0, g_all, acc_gate, out_gate)
    U1.g1()
    Q0.t20()
    G1.rest()
    G1.last()
    Q1.a(0)
    Q1.a(1)
    Q0.s01()
    Q1.a(2)
    Q1.a(3)
    weight(1, 0, g_all, acc_gate, out_gate)
    U1.rest()
    U1.last()
    Q1.c(0)
    Q1.c(1)
    Q1.c(2)
    Q0.tm10()
    Q1.k(0)
    weight(1, 0, u_all, acc_up, out_up)
    Q1.k(1)
    H1.g1()
    weight(1, 1, g_all, acc_gate, out_gate)
    Q1.c(3)
    weight(1, 1, u_all, acc_up, out_up)
    H1.rest()
    Q1.t20()
    Q1.k(2)
    Q0.fin()
    weight(1, 2, u_all, acc_up, out_up)
    weight(1, 3, u_all, acc_up, out_up)
    Q1.k(3)
    Q1.s01()
    H1.last()
    down(1, 0)
    Q1.tm10()
    weight(1, 2, g_all, acc_gate, out_gate)
    weight(1, 3, g_all, acc_gate, out_gate)
    down(1, 1)
    down(1, 2)
    down(1, 3)
    Q1.fin()
    wire.drain()
    assert wire.count == N_MESSAGES, wire.count


def move(*refs):
    sources, results, sems = refs[:4], refs[4:8], refs[8]
    saves = []
    for array in range(4):
        rows = sources[array].shape[0] // 2
        for part in range(2):
            at = pl.ds(part * rows, rows)
            saves.append(
                pltpu.make_async_copy(
                    sources[array].at[at], results[array].at[at], sems.at[2 * array + part]
                )
            )
    for save in saves:
        save.start()
    for save in saves:
        save.wait()


def shards(
    inputs, upstream, mask_flags, levels, gate_saved, up_saved, gate_weight, up_weight, down_weight
):
    anywhere = pl.BlockSpec(memory_space=pl.ANY)
    results = (
        jax.ShapeDtypeStruct((128, 1024), BF),
        jax.ShapeDtypeStruct((1024, 896), BF),
        jax.ShapeDtypeStruct((1024, 896), BF),
        jax.ShapeDtypeStruct((896, 1024), BF),
    )
    inside = pl.BlockSpec(memory_space=pltpu.VMEM)
    grads = pl.pallas_call(
        kernel,
        out_shape=tuple(pltpu.VMEM(result.shape, BF) for result in results),
        in_specs=[
            pl.BlockSpec(memory_space=pltpu.SMEM),
            pl.BlockSpec(memory_space=pltpu.VMEM),
        ]
        + [anywhere] * 7,
        out_specs=(inside,) * 4,
        scratch_shapes=[
            pltpu.VMEM((16, 128, 1024), BF),
            pltpu.VMEM((16, 1024, 128), BF),
            pltpu.VMEM((16, 896, 128), BF),
            pltpu.VMEM((16, 128, 896), BF),
            pltpu.VMEM((16, 128, 896), BF),
            pltpu.VMEM((1024, 896), BF),
            pltpu.VMEM((1024, 896), BF),
            pltpu.VMEM((896, 1024), BF),
            pltpu.VMEM((128, 1024), BF),
            pltpu.VMEM((128, 1024), BF),
            pltpu.VMEM((256, 896), BF),
            pltpu.VMEM((256, 896), BF),
            pltpu.VMEM((2, 8, 128, 896), BF),
            pltpu.VMEM((2, 7, 128, 896), BF),
            pltpu.VMEM((2, 8, 2, 64, 1024), BF),
            pltpu.VMEM((2, 8, 64, 1024), BF),
            pltpu.VMEM((2, 7, 64, 1024), BF),
            pltpu.VMEM((4, 256, 1024), F32),
            pltpu.VMEM((896, 1024), F32),
            pltpu.VMEM((1024, 896), F32),
            pltpu.VMEM((1024, 896), F32),
            pltpu.VMEM((9, 8, 128), F32),
            pltpu.SemaphoreType.DMA((N_MESSAGES,)),
            pltpu.SemaphoreType.DMA((N_MESSAGES,)),
            pltpu.SemaphoreType.DMA((N_LOCAL,)),
        ],
        compiler_params=pltpu.CompilerParams(
            collective_id=0, has_side_effects=True, vmem_limit_bytes=56 * 2**20
        ),
        cost_estimate=pl.CostEstimate(
            flops=12 * 2048 * 1024 * 896, bytes_accessed=16 * 2**20, transcendentals=2 * 256 * 896
        ),
        name="swiglu_backward",
    )(
        levels,
        mask_flags.reshape(1, -1),
        inputs,
        upstream,
        gate_saved,
        up_saved,
        gate_weight,
        up_weight,
        down_weight,
    )
    return pl.pallas_call(
        move,
        out_shape=results,
        in_specs=[inside] * 4,
        out_specs=(anywhere,) * 4,
        scratch_shapes=[pltpu.SemaphoreType.DMA((8,))],
        compiler_params=pltpu.CompilerParams(vmem_limit_bytes=56 * 2**20),
        name="move_results",
    )(*[pltpu.with_memory_space_constraint(grad, pltpu.VMEM) for grad in grads])


def solution(mesh):
    placed = (
        P("row", "col"),
        P("row", "col"),
        P("row"),
        P(),
        P("col", "row"),
        P("col", "row"),
        P("col", "row"),
        P("col", "row"),
        P("row", "col"),
    )
    return jax.shard_map(
        shards,
        mesh=mesh,
        in_specs=placed,
        out_specs=(P("row", "col"), P("col", "row"), P("col", "row"), P("row", "col")),
        check_vma=False,
    )
```
